256 devices in a mesh: section: 8 (over y, z_hi), tensor: 32 (over z_lo, x, core).
Axes of the slice: x: 4, y: 4, z: 8 (z_hi: 2, z_lo: 4; z = z_hi * 4 + z_lo), core: 2. Of those that a mesh axis runs over, the one named last changes fastest.
Arguments:
- acts: bfloat16 [8, 4096, 8192], P('section', 'tensor'), may hold values from -6 to 6
- grad_q: bfloat16 [8, 4096, 8192], P('section', 'tensor'), may hold values from -6 to 6
- grad_v: bfloat16 [8, 4096, 1024], P('section', 'tensor'), may hold values from -6 to 6
- fac_a: bfloat16 [8, 128, 131072], P('section', None, 'tensor'), may hold values from -0.0625 to 0.0625
- fac_bq: bfloat16 [8, 128, 65536], P('section', None, 'tensor'), may hold values from -0.0625 to 0.0625
- fac_bv: bfloat16 [8, 128, 8192], P('section', None, 'tensor'), may hold values from -0.1875 to 0.1875
- seq_tenant: int32 [8, 32], P('section'), may hold values from 0 to 127
- tenant_task: int32 [128], replicated, may hold values from 0 to 31
- section_layer: int32 [8], replicated, may hold values from 0 to 79
- task_emb: bfloat16 [32, 4096], replicated, may hold values from -6 to 6
- layer_emb: bfloat16 [80, 4096], replicated, may hold values from -6 to 6
Outputs:
- grad_a: bfloat16 [4096, 131072], P(None, ('tensor', 'section'))
- grad_bq: bfloat16 [4096, 65536], P(None, ('tensor', 'section'))
- grad_bv: bfloat16 [4096, 8192], P('section', 'tensor')
The draws below stay inside these ranges and needn't reach their ends.
All inputs are finite; a program needn't handle non-finite values.
Results may differ from the reference program's by a relative error of at most 0.0064.
Values may be sent and summed in bfloat16 or wider, within the bound.
A program may use at most 64 MiB of HBM per device.

```python
import math
import jax
import jax.numpy as jnp
from jax import lax

D = 8192
DQ = 8192
DV = 1024
LAYERS = 80
H = 4096
R = 8
TOK_DEV = 128
TENANTS = 128
TASKS = 32
SEQS = 32
SECTION_TOK = 4096
N_SECTION = 8
N_TENSOR = 32


def with_ends(result, stream_key, low, top_value):
    dims = result.shape
    spot = [jax.random.randint(jax.random.fold_in(stream_key, axis), (), 0, dims[axis]) for axis in range(len(dims))]
    result = result.at[tuple(spot)].set(low)
    longest = dims.index(max(dims))
    spot[longest] = (spot[longest] + 1) % dims[longest]
    return result.at[tuple(spot)].set(top_value)


def levels(stream_key, dims, split, smallest, largest):
    factor_of = 1.0
    for position, parts in split:
        draws = jax.random.uniform(jax.random.fold_in(jax.random.fold_in(stream_key, 6), position), (parts,), jnp.float32, smallest / len(split), largest / len(split))
        factor_of = factor_of * jnp.repeat(jnp.exp(draws), dims[position] // parts).reshape((-1,) + (1,) * (len(dims) - 1 - position))
    return factor_of


def centred(stream_key, dims, scale, most, pieces=(), dtype=jnp.bfloat16):
    entries = scale * jax.random.normal(stream_key, dims, jnp.float32)
    if pieces:
        entries = entries * levels(stream_key, dims, pieces, -0.22, 0.18)
    return jnp.clip(entries, -most, most).astype(dtype)


def setup_inputs(seed: int = 0) -> dict:
    streams_of = jax.random.split(jax.random.key(seed), 12)
    acts = centred(streams_of[0], (N_SECTION, SECTION_TOK, D), 1.0, 6.0, ((0, 8), (1, 32)))
    grad_q = centred(streams_of[1], (N_SECTION, SECTION_TOK, DQ), 1.0, 6.0, ((0, 8), (1, 32)))
    grad_v = centred(streams_of[2], (N_SECTION, SECTION_TOK, DV), 1.0, 6.0, ((0, 8), (1, 32)))
    fac_a = centred(streams_of[3], (N_SECTION, TENANTS, D * 2 * R), D ** -0.5, 0.0625, ((0, 8), (2, 32)))
    fac_bq = centred(streams_of[4], (N_SECTION, TENANTS, DQ * R), DQ ** -0.5, 0.0625, ((0, 8), (2, 32)))
    fac_bv = centred(streams_of[5], (N_SECTION, TENANTS, DV * R), DV ** -0.5, 0.1875, ((0, 8), (2, 32)))
    seq_tenant = with_ends(jax.random.randint(streams_of[6], (N_SECTION, SEQS), 0, TENANTS), jax.random.fold_in(streams_of[6], 1), 0, TENANTS - 1).astype(jnp.int32)
    tenant_task = with_ends(jax.random.randint(streams_of[7], (TENANTS,), 0, TASKS), jax.random.fold_in(streams_of[7], 1), 0, TASKS - 1).astype(jnp.int32)
    section_layer = with_ends(jax.random.randint(streams_of[8], (N_SECTION,), 0, LAYERS), jax.random.fold_in(streams_of[8], 1), 0, LAYERS - 1).astype(jnp.int32)
    task_emb = centred(streams_of[9], (TASKS, H), 1.0, 6.0)
    layer_emb = centred(streams_of[10], (LAYERS, H), 1.0, 6.0)
    return {"acts": acts, "grad_q": grad_q, "grad_v": grad_v, "fac_a": fac_a, "fac_bq": fac_bq, "fac_bv": fac_bv, "seq_tenant": seq_tenant, "tenant_task": tenant_task, "section_layer": section_layer, "task_emb": task_emb, "layer_emb": layer_emb}


def reference(acts, grad_q, grad_v, fac_a, fac_bq, fac_bv, seq_tenant, tenant_task, section_layer, task_emb, layer_emb):
    gradient_scale_factor = 2.0 / math.sqrt(TOK_DEV * N_TENSOR * N_SECTION)
    highest_precision_mode = lax.Precision.HIGHEST

    def per_section(section_items):
        section_acts, section_q, section_v, section_a, section_bq, section_bv, owners = section_items
        seq_count = owners.shape[0]
        input_arrays = section_acts.reshape(seq_count, TOK_DEV, D).astype(jnp.float32)
        cotan_query = section_q.reshape(seq_count, TOK_DEV, DQ).astype(jnp.float32)
        cotan_value = section_v.reshape(seq_count, TOK_DEV, DV).astype(jnp.float32)
        down_selected_rows = section_a[owners].reshape(seq_count, D, 2 * R).astype(jnp.float32)
        upq_sel = section_bq[owners].reshape(seq_count, DQ, R).astype(jnp.float32)
        upv_sel = section_bv[owners].reshape(seq_count, DV, R).astype(jnp.float32)
        down_projection_weight = jnp.einsum('kvn,knf->kvf', input_arrays, down_selected_rows, precision=highest_precision_mode)
        back_query = jnp.einsum('sle,ser->slr', cotan_query, upq_sel, precision=highest_precision_mode)
        back_value = jnp.einsum('sle,ser->slr', cotan_value, upv_sel, precision=highest_precision_mode)
        down_round = lax.optimization_barrier(down_projection_weight.astype(jnp.bfloat16)).astype(jnp.float32)
        back_all = jnp.concatenate([back_query, back_value], axis=-1)
        backward_rounded = lax.optimization_barrier(back_all.astype(jnp.bfloat16)).astype(jnp.float32)
        sequence_down_factor = gradient_scale_factor * jnp.einsum('zce,zcg->zeg', input_arrays, backward_rounded, precision=highest_precision_mode)
        seq_bq = gradient_scale_factor * jnp.einsum('sle,slr->ser', cotan_query, down_round[..., :R], precision=highest_precision_mode)
        seq_bv = gradient_scale_factor * jnp.einsum('sle,slr->ser', cotan_value, down_round[..., R:], precision=highest_precision_mode)
        return (sequence_down_factor.reshape(seq_count, -1).astype(jnp.bfloat16), seq_bq.reshape(seq_count, -1).astype(jnp.bfloat16), seq_bv.reshape(seq_count, -1).astype(jnp.bfloat16))
    sequence_down_factor, seq_bq, seq_bv = lax.map(per_section, (acts, grad_q, grad_v, fac_a, fac_bq, fac_bv, seq_tenant))
    task_rows = task_emb[tenant_task].astype(jnp.float32)
    layer_rows = layer_emb[section_layer].astype(jnp.float32)
    head_seq = jax.nn.silu(layer_rows[:, None, :] + task_rows[seq_tenant]).astype(jnp.bfloat16).reshape(-1, H)
    head_t = head_seq.T
    grad_a = jnp.dot(head_t, sequence_down_factor.reshape(-1, D * 2 * R), preferred_element_type=jnp.float32).astype(jnp.bfloat16)
    grad_bq = jnp.dot(head_t, seq_bq.reshape(-1, DQ * R), preferred_element_type=jnp.float32).astype(jnp.bfloat16)
    grad_bv = jnp.dot(head_t, seq_bv.reshape(-1, DV * R), preferred_element_type=jnp.float32).astype(jnp.bfloat16)
    return (grad_a, grad_bq, grad_bv)
```

```python
import functools
import math

import jax
import jax.numpy as jnp
from jax import lax
from jax.experimental import pallas as pl
from jax.experimental.pallas import tpu as pltpu
from jax.sharding import PartitionSpec as P

MESH = pl.DeviceIdType.MESH
F32, BF16 = jnp.float32, jnp.bfloat16

H = 4096
R = 8
TENANTS = 128
TASKS = 32
LAYERS = 80
TOK = 128
NS, NT = 8, 32
NX, NY, NZL, NZH, NC = 4, 4, 4, 2, 2
SCALE = 2.0 / math.sqrt(TOK * NT * NS)


def mm(a, b):
    return jnp.dot(a, b, preferred_element_type=F32)


def iota(shape, dim):
    return lax.broadcasted_iota(jnp.int32, shape, dim)


def exchange(
    acts, gq, gv, fa, fq, fv, own, task_of, layer_of, task_emb, layer_emb,
    s_a, s_q, head_out, head_own,
    acts_v, gq_v, gv_v, fa_v, fq_v, fv_v, emb_v, head_v,
    own_s, own_r, gat_a, gat_q, tr, a2, b2, v2,
    p_as, p_ar, p_qs, p_qr, z_as, z_ar, z_qs, z_qr, x_as, x_qs, big_a, big_q,
    load_sem, out_sem, own_ss, own_rs, pa_ss, pa_rs, pq_ss, pq_rs, za_ss, za_rs, zq_ss, zq_rs, xa_ss, xa_rs, xq_ss, xq_rs,
):
    s, t = lax.axis_index("section"), lax.axis_index("tensor")
    y, zh = s // 2, s % 2
    zl, x, c = t // 8, (t // 2) % 4, t % 2
    zdev = (zl * 2 + zh) * 2 + c
    xy = x * 4 + y

    loads = [
        pltpu.make_async_copy(src, dst, load_sem.at[i])
        for i, (src, dst) in enumerate(
            (
                (fq, fq_v), (fv, fv_v), (fa, fa_v), (gq, gq_v), (gv, gv_v), (acts, acts_v),
                (task_emb, emb_v.at[pl.ds(0, TASKS)]),
                (layer_emb, emb_v.at[pl.ds(TASKS, LAYERS)]),
            )
        )
    ]
    for load in loads:
        load.start()

    bar = pltpu.get_barrier_semaphore()

    def greet(section, tensor):
        pl.semaphore_signal(bar, inc=1, device_id=(section, tensor), device_id_type=MESH)

    def greet_tensor(k, _):
        greet(s, lax.rem(t + k, NT))
        return 0

    lax.fori_loop(1, NT, greet_tensor, 0)

    def greet_z(k, _):
        greet(y * 2 + 1 - zh, ((k // 2) * 4 + x) * 2 + k % 2)
        return 0

    lax.fori_loop(0, NZL * NC, greet_z, 0)

    def greet_xy(k, _):
        greet(lax.rem(y + 1 + k // 4, NY) * 2 + zh, (zl * 4 + k % 4) * 2 + c)
        return 0

    lax.fori_loop(0, (NY - 1) * NX, greet_xy, 0)

    def greet_far(k, _):
        greet(lax.rem(y + k, NY) * 2 + 1 - zh, t)
        return 0

    lax.fori_loop(1, NY, greet_far, 0)

    mine = own[...]
    hot_t = (iota((TENANTS, NT), 0) == mine).astype(F32).astype(BF16)

    def pick(block):
        return lax.dot_general(hot_t, block, (((0,), (0,)), ((), ())), preferred_element_type=F32)

    loads[0].wait()
    loads[1].wait()
    for i in range(8):
        got = pick(fq_v[:, i * 256 : (i + 1) * 256])
        for h in range(2):
            yy, zz = i // 2, i % 2
            gat_q[pl.ds(zz * 8 + yy * 2 + h, NT, stride=32), :] = got[:, h * 128 : (h + 1) * 128]
    got = pick(fv_v[...])
    for h in range(2):
        gat_q[pl.ds(16 + h, NT, stride=32), :] = got[:, h * 128 : (h + 1) * 128]
    for h in range(14):
        gat_q[pl.ds(18 + h, NT, stride=32), :] = jnp.zeros((NT, 128), F32)
    p_qs[...] = gat_q[...].reshape(NT, 32, 128).astype(BF16)
    p_qr[pl.ds(t, 1)] = p_qs[pl.ds(t, 1)]

    own_s[...] = jnp.broadcast_to(jnp.concatenate([mine.astype(F32), jnp.zeros((1, 96), F32)], axis=1), (8, 128))
    own_r[pl.ds(s, 1)] = own_s[...].reshape(1, 8, 128)

    pl.semaphore_wait(bar, (NT - 1) + NZL * NC + (NY - 1) * NX + NY - 1)

    def factor_copy(k, src, dst, send, recv):
        to = lax.rem(t + k, NT)
        return pltpu.make_async_remote_copy(
            src_ref=src.at[to], dst_ref=dst.at[t], send_sem=send.at[k], recv_sem=recv.at[t],
            device_id=(s, to), device_id_type=MESH,
        )

    def factor_arrived(k, dst, send, recv):
        source = lax.rem(t + k, NT)
        pltpu.make_async_remote_copy(
            src_ref=dst.at[source], dst_ref=dst.at[source], send_sem=send.at[k], recv_sem=recv.at[source],
            device_id=(s, source), device_id_type=MESH,
        ).wait_recv()

    def send_q(k, _):
        factor_copy(k, p_qs, p_qr, pq_ss, pq_rs).start()
        return 0

    lax.fori_loop(1, NT, send_q, 0)

    loads[2].wait()
    for i in range(16):
        got = pick(fa_v[:, i * 256 : (i + 1) * 256])
        for h in range(2):
            n = i * 2 + h
            yy, zz, rr = n // 8, (n // 4) % 2, n % 4
            gat_a[pl.ds(zz * 16 + yy * 4 + rr, NT, stride=32), :] = got[:, h * 128 : (h + 1) * 128]
    p_as[...] = gat_a[...].reshape(NT, 32, 128).astype(BF16)
    p_ar[pl.ds(t, 1)] = p_as[pl.ds(t, 1)]

    def send_a(k, _):
        factor_copy(k, p_as, p_ar, pa_ss, pa_rs).start()
        return 0

    lax.fori_loop(1, NT, send_a, 0)

    def own_copy(k):
        to = lax.rem(s + k, NS)
        return pltpu.make_async_remote_copy(
            src_ref=own_s, dst_ref=own_r.at[s], send_sem=own_ss.at[k], recv_sem=own_rs.at[s],
            device_id=(to, t), device_id_type=MESH,
        )

    def send_own(k, _):
        own_copy(k).start()
        return 0

    lax.fori_loop(1, NS, send_own, 0)

    loads[3].wait()

    def turn_q(i, _):
        zl_, c_, xp = i // 4, (i // 2) % 2, i % 2
        base = pl.multiple_of((i % 2) * 512, 512)
        for xi in range(2):
            tt = (zl_ * 4 + xp * 2 + xi) * 2 + c_
            for h in range(2):
                block = gq_v[:, pl.ds(pl.multiple_of(tt * 256 + h * 128, 128), 128)].astype(F32).T
                for yy in range(2):
                    for zz in range(2):
                        tr[pl.ds(base + zz * 256 + xi * 128 + (2 * h + yy) * 32, 32), :] = block[
                            (yy * 2 + zz) * 32 : (yy * 2 + zz + 1) * 32
                        ]
        for zz in range(2):
            row = pl.multiple_of(((zl_ * 2 + zz) * 2 + c_) * 32 + xp * 16, 16)
            for e in range(16):
                b2[pl.ds(row, 16), e * 128 : (e + 1) * 128] = tr[
                    pl.ds(base + zz * 256 + e, 16, stride=16), :
                ].astype(BF16)
        return 0

    lax.fori_loop(0, 16, turn_q, 0, unroll=2)

    loads[4].wait()
    for zl_ in range(4):
        for h in range(2):
            block = gv_v[:, (zl_ * 2 + h) * 128 : (zl_ * 2 + h + 1) * 128].astype(F32).T
            for xx in range(2):
                for c_ in range(2):
                    to = (zl_ * 2 + c_) * 128 + (2 * h + xx) * 32
                    tr[to : to + 32, :] = block[(xx * 2 + c_) * 32 : (xx * 2 + c_ + 1) * 32]
    for g in range(4):
        for e in range(16):
            v2[g * 16 : (g + 1) * 16, e * 128 : (e + 1) * 128] = tr[pl.ds(g * 256 + e, 16, stride=16), :].astype(BF16)

    loads[5].wait()

    def turn_a(i, _):
        base = pl.multiple_of((i % 4) * 256, 256)
        zl_, x_, c_ = i // 8, (i // 2) % 4, i % 2
        for h in range(2):
            block = acts_v[:, pl.ds(pl.multiple_of(i * 256 + h * 128, 128), 128)].astype(F32).T
            for yy in range(2):
                for zz in range(2):
                    tr[pl.ds(base + zz * 128 + (2 * h + yy) * 32, 32), :] = block[
                        (yy * 2 + zz) * 32 : (yy * 2 + zz + 1) * 32
                    ]
        for zz in range(2):
            row = pl.multiple_of((((zl_ * 2 + zz) * 2 + c_) * 4 + x_) * 16, 16)
            for d in range(8):
                a2[pl.ds(row, 16), d * 128 : (d + 1) * 128] = tr[pl.ds(base + zz * 128 + d, 16, stride=8), :].astype(BF16)
        return 0

    lax.fori_loop(0, 32, turn_a, 0, unroll=4)

    def got_q(k, _):
        factor_arrived(k, p_qr, pq_ss, pq_rs)
        return 0

    lax.fori_loop(1, NT, got_q, 0)

    places = [(zl_, zz, c_, x_) for zl_ in range(4) for zz in range(2) for c_ in range(2) for x_ in range(4)]
    backq = jnp.zeros((R, TOK), F32)
    fq_rows = jnp.concatenate(
        [p_qr[(zl_ * 4 + x_) * 2 + c_, 0:16, :].astype(F32)[zz * 8 : (zz + 1) * 8] for zl_, zz, c_, x_ in places], axis=0
    )
    fq_t = fq_rows.T.astype(BF16)
    for n in range(8):
        part = mm(fq_t[n * 16 : (n + 1) * 16], b2[:, n * 256 : (n + 1) * 256])
        backq = backq + part[0:8, 0:128] + part[8:16, 128:256]
    fv_rows = jnp.concatenate(
        [p_qr[(zl_ * 4 + x_) * 2 + c_, 16:32, :].astype(F32)[0:2] for zl_ in range(4) for c_ in range(2) for x_ in range(4)],
        axis=0,
    )
    fv_t = jnp.concatenate([fv_rows, jnp.zeros((64, 128), F32)], axis=0).T.astype(BF16)[:, 0:64]
    backv = jnp.zeros((R, TOK), F32)
    for n in range(8):
        part = mm(fv_t[n * 16 : (n + 1) * 16], v2[:, n * 256 : (n + 1) * 256])
        backv = backv + part[0:8, 0:128] + part[8:16, 128:256]
    back_t = jnp.concatenate([backq, backv], axis=0).astype(BF16).astype(F32)
    back = jnp.concatenate([back_t] * 8, axis=0).T
    lane = iota((TOK, 128), 1)
    diag = jnp.concatenate([jnp.where(lane // 16 == d, back, 0.0).astype(BF16) for d in range(8)], axis=0)

    def z_peer(k):
        q = lax.rem(zdev + k, 16)
        return q, (y * 2 + (q // 2) % 2, ((q // 4) * 4 + x) * 2 + q % 2)

    def z_copy(k, src, dst, send, recv):
        q, device = z_peer(k)
        return pltpu.make_async_remote_copy(
            src_ref=src.at[q], dst_ref=dst.at[zdev], send_sem=send.at[k], recv_sem=recv.at[zdev],
            device_id=device, device_id_type=MESH,
        )

    def z_arrived(k, dst, send, recv):
        q, device = z_peer(k)
        pltpu.make_async_remote_copy(
            src_ref=dst.at[q], dst_ref=dst.at[q], send_sem=send.at[k], recv_sem=recv.at[q],
            device_id=device, device_id_type=MESH,
        ).wait_recv()

    for n in range(4):
        z_as[n * 4 : (n + 1) * 4] = (SCALE * mm(a2[n * 256 : (n + 1) * 256, :], diag)).astype(BF16).reshape(4, 64, 128)

    def send_za(k, _):
        z_copy(k, z_as, z_ar, za_ss, za_rs).start()
        return 0

    lax.fori_loop(1, 16, send_za, 0)
    z_ar[pl.ds(zdev, 1)] = z_as[pl.ds(zdev, 1)]

    def got_a(k, _):
        factor_arrived(k, p_ar, pa_ss, pa_rs)
        return 0

    lax.fori_loop(1, NT, got_a, 0)
    fa_rows = jnp.concatenate([p_ar[(zl_ * 4 + x_) * 2 + c_, zz * 16 : (zz + 1) * 16, :] for zl_, zz, c_, x_ in places], axis=0)
    fa_t = fa_rows.astype(F32).T.astype(BF16)
    down_t = jnp.zeros((2 * R, TOK), F32)
    for n in range(4):
        part = mm(fa_t[n * 32 : (n + 1) * 32], a2[:, n * 256 : (n + 1) * 256])
        down_t = down_t + part[0:16, 0:128] + part[16:32, 128:256]
    down_t = down_t.astype(BF16).astype(F32)
    down_q = jnp.concatenate([down_t[0:8]] * 16, axis=0).T
    down_v = jnp.concatenate([down_t[8:16]] * 16, axis=0).T
    diag_q = jnp.concatenate([jnp.where(lane // 8 == e, down_q, 0.0).astype(BF16) for e in range(16)], axis=0)
    diag_v = jnp.concatenate([jnp.where(lane // 8 == e, down_v, 0.0).astype(BF16) for e in range(16)], axis=0)
    grad_v_rows = SCALE * mm(v2[...], diag_v)
    grad_v_rows = jnp.concatenate(
        [grad_v_rows.reshape(8, 8, 128), jnp.zeros((8, 8, 128), F32)], axis=1
    ).astype(BF16)
    grad_q_rows = (SCALE * mm(b2[...], diag_q)).astype(BF16).reshape(16, 32, 128)
    for q in range(16):
        z_qs[q, 0:32, :] = grad_q_rows[q]
        z_qs[q, 32:48, :] = grad_v_rows[(q // 4) * 2 + q % 2]

    def send_zq(k, _):
        z_copy(k, z_qs, z_qr, zq_ss, zq_rs).start()
        return 0

    lax.fori_loop(1, 16, send_zq, 0)
    z_qr[pl.ds(zdev, 1)] = z_qs[pl.ds(zdev, 1)]

    def got_own(k, _):
        source = lax.rem(s + k, NS)
        pltpu.make_async_remote_copy(
            src_ref=own_s, dst_ref=own_r.at[source], send_sem=own_ss.at[k], recv_sem=own_rs.at[source],
            device_id=(source, t), device_id_type=MESH,
        ).wait_recv()
        return 0

    lax.fori_loop(1, NS, got_own, 0)
    n_seq = NS * NT
    col = iota((1, n_seq), 1)
    col_s = (col // 16 % 4) * 2 + (col // 2) % 2
    col_t = ((col // 4 % 4) * 4 + col // 64) * 2 + col % 2
    owners = jnp.concatenate([own_r[i, 0:1, :] for i in range(NS)], axis=0)
    spread = mm(owners.astype(BF16), (iota((128, n_seq), 0) == col_t).astype(F32).astype(BF16))
    in_section = iota((NS, n_seq), 0) == col_s
    tenant = jnp.sum(jnp.where(in_section, spread, 0.0), axis=0, keepdims=True)
    hot_tenant = (iota((TENANTS, n_seq), 0).astype(F32) == tenant).astype(F32).astype(BF16)
    tasks = jnp.broadcast_to(task_of[...].astype(F32), (8, TENANTS)).astype(BF16)
    task = mm(tasks, hot_tenant)[0:1]
    layers = jnp.broadcast_to(layer_of[...].astype(F32), (NS, NS)).astype(BF16)
    layer = mm(layers, in_section.astype(F32).astype(BF16))[0:1]
    row = iota((TASKS + LAYERS, n_seq), 0).astype(F32)
    hot_head = (row == jnp.where(row < TASKS, task, layer + TASKS)).astype(F32).astype(BF16)
    loads[6].wait()
    loads[7].wait()

    def head_block(i, _):
        at = pl.multiple_of(i * 256, 256)
        v = lax.dot_general(
            emb_v[:, pl.ds(at, 256)], hot_head, (((0,), (0,)), ((), ())), preferred_element_type=F32
        )
        head_v[pl.ds(at, 256), :] = (v / (1.0 + jnp.exp(-v))).astype(BF16)
        return 0

    lax.fori_loop(0, H // 256, head_block, 0)
    share = H // NS
    head_copy = pltpu.make_async_copy(head_v, head_out, out_sem.at[0])
    own_head_copy = pltpu.make_async_copy(
        head_v.at[pl.ds(pl.multiple_of(s * share, share), share)], head_own, out_sem.at[1]
    )
    head_copy.start()
    own_head_copy.start()

    def xy_copy(k, src, dst, send, recv):
        b = lax.rem(xy + k, 16)
        return pltpu.make_async_remote_copy(
            src_ref=src.at[b], dst_ref=dst.at[xy], send_sem=send.at[k], recv_sem=recv.at[xy],
            device_id=((b % 4) * 2 + zh, (zl * 4 + b // 4) * 2 + c), device_id_type=MESH,
        )

    def xy_arrived(k, dst, send, recv):
        b = lax.rem(xy + k, 16)
        pltpu.make_async_remote_copy(
            src_ref=dst.at[b], dst_ref=dst.at[b], send_sem=send.at[k], recv_sem=recv.at[b],
            device_id=((b % 4) * 2 + zh, (zl * 4 + b // 4) * 2 + c), device_id_type=MESH,
        ).wait_recv()

    def got_za(k, _):
        z_arrived(k, z_ar, za_ss, za_rs)
        return 0

    lax.fori_loop(1, 16, got_za, 0)
    big_a[...] = z_ar[...].astype(F32).reshape(1024, 128)
    for b in range(16):
        for i in range(4):
            x_as[b, :, i * 128 : (i + 1) * 128] = big_a[pl.ds(b * 4 + i, 16, stride=64), :].astype(BF16)

    def send_xa(k, _):
        xy_copy(k, x_as, s_a, xa_ss, xa_rs).start()
        return 0

    lax.fori_loop(1, 16, send_xa, 0)
    s_a[pl.ds(xy, 1)] = x_as[pl.ds(xy, 1)]

    def got_zq(k, _):
        z_arrived(k, z_qr, zq_ss, zq_rs)
        return 0

    lax.fori_loop(1, 16, got_zq, 0)
    big_q[...] = z_qr[...].astype(F32).reshape(768, 128)
    for b in range(16):
        for i in range(2):
            x_qs[b, :, i * 128 : (i + 1) * 128] = big_q[pl.ds(b * 2 + i, 16, stride=48), :].astype(BF16)
            x_qs[b, :, 256 + i * 128 : 256 + (i + 1) * 128] = big_q[
                pl.ds(32 + (b // 4) * 2 + i, 16, stride=48), :
            ].astype(BF16)

    def send_xq(k, _):
        xy_copy(k, x_qs, s_q, xq_ss, xq_rs).start()
        return 0

    lax.fori_loop(1, 16, send_xq, 0)
    s_q[pl.ds(xy, 1)] = x_qs[pl.ds(xy, 1)]

    def sent_factors(k, _):
        factor_copy(k, p_qs, p_qr, pq_ss, pq_rs).wait_send()
        factor_copy(k, p_as, p_ar, pa_ss, pa_rs).wait_send()
        return 0

    lax.fori_loop(1, NT, sent_factors, 0)

    def sent_own(k, _):
        own_copy(k).wait_send()
        return 0

    lax.fori_loop(1, NS, sent_own, 0)

    def sent_z(k, _):
        z_copy(k, z_as, z_ar, za_ss, za_rs).wait_send()
        z_copy(k, z_qs, z_qr, zq_ss, zq_rs).wait_send()
        return 0

    lax.fori_loop(1, 16, sent_z, 0)
    head_copy.wait()
    own_head_copy.wait()

    def done_xy(k, _):
        xy_arrived(k, s_a, xa_ss, xa_rs)
        xy_arrived(k, s_q, xq_ss, xq_rs)
        xy_copy(k, x_as, s_a, xa_ss, xa_rs).wait_send()
        xy_copy(k, x_qs, s_q, xq_ss, xq_rs).wait_send()
        return 0

    lax.fori_loop(1, 16, done_xy, 0)


def head_product(head, s_a, s_q, head_own, grad_a, grad_bq, grad_bv):
    rows = head[...]
    grad_a[...] = mm(rows, s_a[...]).astype(BF16)
    grad_bq[...] = mm(rows, s_q[:, 0:256]).astype(BF16)

    @pl.when(pl.program_id(0) == 0)
    def _():
        grad_bv[...] = mm(head_own[...], s_q[:, 256:512]).astype(BF16)


def shards(acts, grad_q, grad_v, fac_a, fac_bq, fac_bv, seq_tenant, tenant_task, section_layer, task_emb, layer_emb):
    vmem = pl.BlockSpec(memory_space=pltpu.VMEM)
    anywhere = pl.BlockSpec(memory_space=pl.ANY)
    dma = pltpu.SemaphoreType.DMA
    s_a, s_q, head, head_own = pl.pallas_call(
        exchange,
        out_shape=(
            jax.ShapeDtypeStruct((16, 16, 512), BF16),
            jax.ShapeDtypeStruct((16, 16, 512), BF16),
            jax.ShapeDtypeStruct((H, NS * NT), BF16),
            jax.ShapeDtypeStruct((H // NS, NS * NT), BF16),
        ),
        in_specs=[anywhere] * 6 + [vmem] * 3 + [anywhere] * 2,
        out_specs=(vmem, vmem, anywhere, anywhere),
        scratch_shapes=[
            pltpu.VMEM((TOK, 8192), BF16),
            pltpu.VMEM((TOK, 8192), BF16),
            pltpu.VMEM((TOK, 1024), BF16),
            pltpu.VMEM((TENANTS, 4096), BF16),
            pltpu.VMEM((TENANTS, 2048), BF16),
            pltpu.VMEM((TENANTS, 256), BF16),
            pltpu.VMEM((TASKS + LAYERS, H), BF16),
            pltpu.VMEM((H, NS * NT), BF16),
            pltpu.VMEM((8, 128), F32),
            pltpu.VMEM((NS, 8, 128), F32),
            pltpu.VMEM((NT * 32, 128), F32),
            pltpu.VMEM((NT * 32, 128), F32),
            pltpu.VMEM((1024, 128), F32),
            pltpu.VMEM((1024, 1024), BF16),
            pltpu.VMEM((512, 2048), BF16),
            pltpu.VMEM((64, 2048), BF16),
            pltpu.VMEM((NT, 32, 128), BF16),
            pltpu.VMEM((NT, 32, 128), BF16),
            pltpu.VMEM((NT, 32, 128), BF16),
            pltpu.VMEM((NT, 32, 128), BF16),
            pltpu.VMEM((16, 64, 128), BF16),
            pltpu.VMEM((16, 64, 128), BF16),
            pltpu.VMEM((16, 48, 128), BF16),
            pltpu.VMEM((16, 48, 128), BF16),
            pltpu.VMEM((16, 16, 512), BF16),
            pltpu.VMEM((16, 16, 512), BF16),
            pltpu.VMEM((1024, 128), F32),
            pltpu.VMEM((768, 128), F32),
            dma((8,)), dma((2,)),
            dma((NS,)), dma((NS,)),
            dma((NT,)), dma((NT,)), dma((NT,)), dma((NT,)),
            dma((16,)), dma((16,)), dma((16,)), dma((16,)),
            dma((16,)), dma((16,)), dma((16,)), dma((16,)),
        ],
        compiler_params=pltpu.CompilerParams(
            collective_id=0, has_side_effects=True, vmem_limit_bytes=56 * 1024 * 1024
        ),
        name="exchange",
    )(
        acts[0], grad_q[0], grad_v[0], fac_a[0], fac_bq[0], fac_bv[0], seq_tenant,
        tenant_task.reshape(1, TENANTS), section_layer.reshape(1, NS), task_emb, layer_emb,
    )
    tile = 512
    return pl.pallas_call(
        head_product,
        grid=(H // tile,),
        out_shape=(
            jax.ShapeDtypeStruct((H, 512), BF16),
            jax.ShapeDtypeStruct((H, 256), BF16),
            jax.ShapeDtypeStruct((H // NS, 256), BF16),
        ),
        in_specs=[
            pl.BlockSpec((tile, 256), lambda i: (i, 0)),
            pl.BlockSpec((256, 512), lambda i: (0, 0)),
            pl.BlockSpec((256, 512), lambda i: (0, 0)),
            pl.BlockSpec((512, 256), lambda i: (0, 0)),
        ],
        out_specs=(
            pl.BlockSpec((tile, 512), lambda i: (i, 0)),
            pl.BlockSpec((tile, 256), lambda i: (i, 0)),
            pl.BlockSpec((512, 256), lambda i: (0, 0)),
        ),
        compiler_params=pltpu.CompilerParams(vmem_limit_bytes=60 * 1024 * 1024),
        name="head_product",
    )(head, s_a.reshape(256, 512), s_q.reshape(256, 512), head_own)


def solution(mesh):
    placed = (
        P("section", "tensor", None),
        P("section", "tensor", None),
        P("section", "tensor", None),
        P("section", None, "tensor"),
        P("section", None, "tensor"),
        P("section", None, "tensor"),
        P("section", None),
        P(),
        P(),
        P(),
        P(),
    )
    return jax.shard_map(
        shards,
        mesh=mesh,
        in_specs=placed,
        out_specs=(
            P(None, ("tensor", "section")),
            P(None, ("tensor", "section")),
            P("section", "tensor"),
        ),
        check_vma=False,
    )
```

```python
import functools
import math

import jax
import jax.numpy as jnp
from jax import lax
from jax.experimental import pallas as pl
from jax.experimental.pallas import tpu as pltpu
from jax.sharding import PartitionSpec as P

MESH = pl.DeviceIdType.MESH
F32, BF16 = jnp.float32, jnp.bfloat16

H = 4096
R = 8
TENANTS = 128
TASKS = 32
LAYERS = 80
TOK = 128
NS, NT = 8, 32
NX, NY, NZL, NZH, NC = 4, 4, 4, 2, 2
HEAD_FIRST = 8
PIECES = 4
SCALE = 2.0 / math.sqrt(TOK * NT * NS)


def mm(a, b):
    return jnp.dot(a, b, preferred_element_type=F32)


def iota(shape, dim):
    return lax.broadcasted_iota(jnp.int32, shape, dim)


def exchange(
    acts, gq, gv, fa, fq, fv, own, task_of, layer_of, task_emb, layer_emb,
    s_a, s_q, head, head_own,
    acts_v, gq_v, gv_v, fa_v, fq_v, fv_v, emb_v, own_v, task_v, layer_v,
    own_s, own_r, gat_a, gat_q, tr, a2, b2, v2,
    p_as, p_ar, p_qs, p_qr, z_as, z_ar, z_qs, z_qr, x_as, x_qs, big_a, big_q,
    load_sem, own_ss, own_rs, pa_ss, pa_rs, pq_ss, pq_rs, za_ss, za_rs, zq_ss, zq_rs, xa_ss, xa_rs, xq_ss, xq_rs,
):
    s, t = lax.axis_index("section"), lax.axis_index("tensor")
    y, zh = s // 2, s % 2
    zl, x, c = t // 8, (t // 2) % 4, t % 2
    zdev = (zl * 2 + zh) * 2 + c
    xy = x * 4 + y

    bar = pltpu.get_barrier_semaphore()

    def greet(section, tensor):
        pl.semaphore_signal(bar, inc=1, device_id=(section, tensor), device_id_type=MESH)

    def greet_tensor(k, _):
        greet(s, lax.rem(t + k, NT))
        return 0

    lax.fori_loop(1, NT, greet_tensor, 0)

    def greet_z(k, _):
        greet(y * 2 + 1 - zh, ((k // 2) * 4 + x) * 2 + k % 2)
        return 0

    lax.fori_loop(0, NZL * NC, greet_z, 0)

    def greet_xy(k, _):
        greet(lax.rem(y + 1 + k // 4, NY) * 2 + zh, (zl * 4 + k % 4) * 2 + c)
        return 0

    lax.fori_loop(0, (NY - 1) * NX, greet_xy, 0)

    def greet_far(k, _):
        greet(lax.rem(y + k, NY) * 2 + 1 - zh, t)
        return 0

    lax.fori_loop(1, NY, greet_far, 0)

    loads = [
        pltpu.make_async_copy(src, dst, load_sem.at[i])
        for i, (src, dst) in enumerate(
            (
                (own, own_v), (fq, fq_v), (fv, fv_v), (fa, fa_v), (gq, gq_v), (gv, gv_v), (acts, acts_v),
                (task_emb, emb_v.at[pl.ds(0, TASKS)]),
                (layer_emb, emb_v.at[pl.ds(TASKS, LAYERS)]),
                (task_of, task_v), (layer_of, layer_v),
            )
        )
    ]
    for load in loads:
        load.start()

    loads[0].wait()
    mine = own_v[...]
    hot_t = (iota((TENANTS, NT), 0) == mine).astype(F32).astype(BF16)

    def pick(block):
        return lax.dot_general(hot_t, block, (((0,), (0,)), ((), ())), preferred_element_type=F32)

    loads[1].wait()
    loads[2].wait()
    for i in range(8):
        got = pick(fq_v[:, i * 256 : (i + 1) * 256])
        for h in range(2):
            yy, zz = i // 2, i % 2
            gat_q[pl.ds(zz * 8 + yy * 2 + h, NT, stride=24), :] = got[:, h * 128 : (h + 1) * 128]
    got = pick(fv_v[...])
    for h in range(2):
        gat_q[pl.ds(16 + h, NT, stride=24), :] = got[:, h * 128 : (h + 1) * 128]
    for h in range(6):
        gat_q[pl.ds(18 + h, NT, stride=24), :] = jnp.zeros((NT, 128), F32)
    p_qs[...] = gat_q[...].reshape(NT, 24, 128).astype(BF16)
    p_qr[pl.ds(t, 1)] = p_qs[pl.ds(t, 1)]

    own_s[...] = jnp.broadcast_to(jnp.concatenate([mine.astype(F32), jnp.zeros((1, 96), F32)], axis=1), (8, 128))
    own_r[pl.ds(s, 1)] = own_s[...].reshape(1, 8, 128)

    pl.semaphore_wait(bar, (NT - 1) + NZL * NC + (NY - 1) * NX + NY - 1)

    def factor_copy(k, src, dst, send, recv):
        to = lax.rem(t + k, NT)
        return pltpu.make_async_remote_copy(
            src_ref=src.at[to], dst_ref=dst.at[t], send_sem=send.at[k], recv_sem=recv.at[t],
            device_id=(s, to), device_id_type=MESH,
        )

    def factor_arrived(k, dst, send, recv):
        source = lax.rem(t + k, NT)
        pltpu.make_async_remote_copy(
            src_ref=dst.at[source], dst_ref=dst.at[source], send_sem=send.at[k], recv_sem=recv.at[source],
            device_id=(s, source), device_id_type=MESH,
        ).wait_recv()

    def own_copy(k):
        to = lax.rem(s + k, NS)
        return pltpu.make_async_remote_copy(
            src_ref=own_s, dst_ref=own_r.at[s], send_sem=own_ss.at[k], recv_sem=own_rs.at[s],
            device_id=(to, t), device_id_type=MESH,
        )

    def send_own(k, _):
        own_copy(k).start()
        return 0

    lax.fori_loop(1, NS, send_own, 0)

    def send_q(k, _):
        factor_copy(k, p_qs, p_qr, pq_ss, pq_rs).start()
        return 0

    lax.fori_loop(1, NT, send_q, 0)

    loads[3].wait()
    for i in range(16):
        got = pick(fa_v[:, i * 256 : (i + 1) * 256])
        for h in range(2):
            n = i * 2 + h
            yy, zz, rr = n // 8, (n // 4) % 2, n % 4
            gat_a[pl.ds(zz * 16 + yy * 4 + rr, NT, stride=32), :] = got[:, h * 128 : (h + 1) * 128]
    p_as[...] = gat_a[...].reshape(NT, 32, 128).astype(BF16)
    p_ar[pl.ds(t, 1)] = p_as[pl.ds(t, 1)]

    def send_a(k, _):
        factor_copy(k, p_as, p_ar, pa_ss, pa_rs).start()
        return 0

    lax.fori_loop(1, NT, send_a, 0)

    loads[4].wait()

    def turn_q(i, _):
        zl_, c_, xp = i // 4, (i // 2) % 2, i % 2
        base = pl.multiple_of((i % 2) * 512, 512)
        for xi in range(2):
            tt = (zl_ * 4 + xp * 2 + xi) * 2 + c_
            for h in range(2):
                block = gq_v[:, pl.ds(pl.multiple_of(tt * 256 + h * 128, 128), 128)].astype(F32).T
                for yy in range(2):
                    for zz in range(2):
                        tr[pl.ds(base + zz * 256 + xi * 128 + (2 * h + yy) * 32, 32), :] = block[
                            (yy * 2 + zz) * 32 : (yy * 2 + zz + 1) * 32
                        ]
        for zz in range(2):
            row = pl.multiple_of(((zl_ * 2 + zz) * 2 + c_) * 32 + xp * 16, 16)
            for e in range(16):
                b2[pl.ds(row, 16), e * 128 : (e + 1) * 128] = tr[
                    pl.ds(base + zz * 256 + e, 16, stride=16), :
                ].astype(BF16)
        return 0

    lax.fori_loop(0, 16, turn_q, 0, unroll=2)

    loads[5].wait()
    for zl_ in range(4):
        for h in range(2):
            block = gv_v[:, (zl_ * 2 + h) * 128 : (zl_ * 2 + h + 1) * 128].astype(F32).T
            for xx in range(2):
                for c_ in range(2):
                    to = (zl_ * 2 + c_) * 128 + (2 * h + xx) * 32
                    tr[to : to + 32, :] = block[(xx * 2 + c_) * 32 : (xx * 2 + c_ + 1) * 32]
    for g in range(4):
        for e in range(16):
            v2[g * 16 : (g + 1) * 16, e * 128 : (e + 1) * 128] = tr[pl.ds(g * 256 + e, 16, stride=16), :].astype(BF16)

    loads[6].wait()

    def turn_a(i, _):
        base = pl.multiple_of((i % 4) * 256, 256)
        zl_, x_, c_ = i // 8, (i // 2) % 4, i % 2
        for h in range(2):
            block = acts_v[:, pl.ds(pl.multiple_of(i * 256 + h * 128, 128), 128)].astype(F32).T
            for yy in range(2):
                for zz in range(2):
                    tr[pl.ds(base + zz * 128 + (2 * h + yy) * 32, 32), :] = block[
                        (yy * 2 + zz) * 32 : (yy * 2 + zz + 1) * 32
                    ]
        for zz in range(2):
            row = pl.multiple_of((((zl_ * 2 + zz) * 2 + c_) * 4 + x_) * 16, 16)
            for d in range(8):
                a2[pl.ds(row, 16), d * 128 : (d + 1) * 128] = tr[pl.ds(base + zz * 128 + d, 16, stride=8), :].astype(BF16)
        return 0

    lax.fori_loop(0, 32, turn_a, 0, unroll=4)

    def got_q(k, _):
        factor_arrived(k, p_qr, pq_ss, pq_rs)
        return 0

    lax.fori_loop(1, NT, got_q, 0)

    places = [(zl_, zz, c_, x_) for zl_ in range(4) for zz in range(2) for c_ in range(2) for x_ in range(4)]
    backq = jnp.zeros((R, TOK), F32)
    fq_rows = jnp.concatenate(
        [p_qr[(zl_ * 4 + x_) * 2 + c_, 0:16, :].astype(F32)[zz * 8 : (zz + 1) * 8] for zl_, zz, c_, x_ in places], axis=0
    )
    fq_t = fq_rows.T.astype(BF16)
    for n in range(8):
        part = mm(fq_t[n * 16 : (n + 1) * 16], b2[:, n * 256 : (n + 1) * 256])
        backq = backq + part[0:8, 0:128] + part[8:16, 128:256]
    fv_rows = jnp.concatenate(
        [p_qr[(zl_ * 4 + x_) * 2 + c_, 16:24, :].astype(F32)[0:2] for zl_ in range(4) for c_ in range(2) for x_ in range(4)],
        axis=0,
    )
    fv_t = jnp.concatenate([fv_rows, jnp.zeros((64, 128), F32)], axis=0).T.astype(BF16)[:, 0:64]
    backv = jnp.zeros((R, TOK), F32)
    for n in range(8):
        part = mm(fv_t[n * 16 : (n + 1) * 16], v2[:, n * 256 : (n + 1) * 256])
        backv = backv + part[0:8, 0:128] + part[8:16, 128:256]
    back_t = jnp.concatenate([backq, backv], axis=0).astype(BF16).astype(F32)
    back = jnp.concatenate([back_t] * 8, axis=0).T
    lane = iota((TOK, 128), 1)
    diag = jnp.concatenate([jnp.where(lane // 16 == d, back, 0.0).astype(BF16) for d in range(8)], axis=0)

    def z_peer(k):
        q = lax.rem(zdev + k, 16)
        return q, (y * 2 + (q // 2) % 2, ((q // 4) * 4 + x) * 2 + q % 2)

    def z_copy(k, src, dst, send, recv):
        q, device = z_peer(k)
        return pltpu.make_async_remote_copy(
            src_ref=src.at[q], dst_ref=dst.at[zdev], send_sem=send.at[k], recv_sem=recv.at[zdev],
            device_id=device, device_id_type=MESH,
        )

    def z_arrived(k, dst, send, recv):
        q, device = z_peer(k)
        pltpu.make_async_remote_copy(
            src_ref=dst.at[q], dst_ref=dst.at[q], send_sem=send.at[k], recv_sem=recv.at[q],
            device_id=device, device_id_type=MESH,
        ).wait_recv()

    for n in range(4):
        z_as[n * 4 : (n + 1) * 4] = (SCALE * mm(a2[n * 256 : (n + 1) * 256, :], diag)).astype(BF16).reshape(4, 64, 128)

    def send_za(k, _):
        z_copy(k, z_as, z_ar, za_ss, za_rs).start()
        return 0

    lax.fori_loop(1, 16, send_za, 0)
    z_ar[pl.ds(zdev, 1)] = z_as[pl.ds(zdev, 1)]

    def got_own(k, _):
        source = lax.rem(s + k, NS)
        pltpu.make_async_remote_copy(
            src_ref=own_s, dst_ref=own_r.at[source], send_sem=own_ss.at[k], recv_sem=own_rs.at[source],
            device_id=(source, t), device_id_type=MESH,
        ).wait_recv()
        return 0

    lax.fori_loop(1, NS, got_own, 0)
    for i in (7, 8, 9, 10):
        loads[i].wait()
    n_seq = NS * NT
    col = iota((1, n_seq), 1)
    col_s = (col // 16 % 4) * 2 + (col // 2) % 2
    col_t = ((col // 4 % 4) * 4 + col // 64) * 2 + col % 2
    owners = jnp.concatenate([own_r[i, 0:1, :] for i in range(NS)], axis=0)
    spread = mm(owners.astype(BF16), (iota((128, n_seq), 0) == col_t).astype(F32).astype(BF16))
    in_section = iota((NS, n_seq), 0) == col_s
    tenant = jnp.sum(jnp.where(in_section, spread, 0.0), axis=0, keepdims=True)
    hot_tenant = (iota((TENANTS, n_seq), 0).astype(F32) == tenant).astype(F32).astype(BF16)
    tasks = jnp.broadcast_to(task_v[...].astype(F32), (8, TENANTS)).astype(BF16)
    task = mm(tasks, hot_tenant)[0:1]
    layers = jnp.broadcast_to(layer_v[...].astype(F32), (NS, NS)).astype(BF16)
    layer = mm(layers, in_section.astype(F32).astype(BF16))[0:1]
    row = iota((TASKS + LAYERS, n_seq), 0).astype(F32)
    hot_head = (row == jnp.where(row < TASKS, task, layer + TASKS)).astype(F32).astype(BF16)

    def head_block(i, _):
        at = pl.multiple_of(i * 256, 256)
        v = lax.dot_general(
            emb_v[:, pl.ds(at, 256)], hot_head, (((0,), (0,)), ((), ())), preferred_element_type=F32
        )
        head[pl.ds(at, 256), :] = (v / (1.0 + jnp.exp(-v))).astype(BF16)
        return 0

    lax.fori_loop(0, HEAD_FIRST, head_block, 0)

    def got_a(k, _):
        factor_arrived(k, p_ar, pa_ss, pa_rs)
        return 0

    lax.fori_loop(1, NT, got_a, 0)
    fa_rows = jnp.concatenate([p_ar[(zl_ * 4 + x_) * 2 + c_, zz * 16 : (zz + 1) * 16, :] for zl_, zz, c_, x_ in places], axis=0)
    fa_t = fa_rows.astype(F32).T.astype(BF16)
    down_t = jnp.zeros((2 * R, TOK), F32)
    for n in range(4):
        part = mm(fa_t[n * 32 : (n + 1) * 32], a2[:, n * 256 : (n + 1) * 256])
        down_t = down_t + part[0:16, 0:128] + part[16:32, 128:256]
    down_t = down_t.astype(BF16).astype(F32)
    down_q = jnp.concatenate([down_t[0:8]] * 16, axis=0).T
    down_v = jnp.concatenate([down_t[8:16]] * 16, axis=0).T
    diag_q = jnp.concatenate([jnp.where(lane // 8 == e, down_q, 0.0).astype(BF16) for e in range(16)], axis=0)
    diag_v = jnp.concatenate([jnp.where(lane // 8 == e, down_v, 0.0).astype(BF16) for e in range(16)], axis=0)
    grad_v_rows = SCALE * mm(v2[...], diag_v)
    grad_v_rows = grad_v_rows.reshape(8, 8, 128).astype(BF16)
    grad_q_rows = (SCALE * mm(b2[...], diag_q)).astype(BF16).reshape(16, 32, 128)
    for q in range(16):
        z_qs[q, 0:32, :] = grad_q_rows[q]
        z_qs[q, 32:40, :] = grad_v_rows[(q // 4) * 2 + q % 2]

    def send_zq(k, _):
        z_copy(k, z_qs, z_qr, zq_ss, zq_rs).start()
        return 0

    lax.fori_loop(1, 16, send_zq, 0)
    z_qr[pl.ds(zdev, 1)] = z_qs[pl.ds(zdev, 1)]

    lax.fori_loop(HEAD_FIRST, H // 256, head_block, 0)
    share = H // NS
    head_own[...] = head[pl.ds(pl.multiple_of(s * share, share), share), :]

    def xy_copy(k, src, dst, send, recv):
        b = lax.rem(xy + k, 16)
        return pltpu.make_async_remote_copy(
            src_ref=src.at[b], dst_ref=dst.at[xy], send_sem=send.at[k], recv_sem=recv.at[xy],
            device_id=((b % 4) * 2 + zh, (zl * 4 + b // 4) * 2 + c), device_id_type=MESH,
        )

    def xy_arrived(k, dst, send, recv):
        b = lax.rem(xy + k, 16)
        pltpu.make_async_remote_copy(
            src_ref=dst.at[b], dst_ref=dst.at[b], send_sem=send.at[k], recv_sem=recv.at[b],
            device_id=((b % 4) * 2 + zh, (zl * 4 + b // 4) * 2 + c), device_id_type=MESH,
        ).wait_recv()

    def got_za(k, _):
        z_arrived(k, z_ar, za_ss, za_rs)
        return 0

    lax.fori_loop(1, 16, got_za, 0)
    big_a[...] = z_ar[...].astype(F32).reshape(1024, 128)
    for b in range(16):
        for i in range(4):
            x_as[b, :, i * 128 : (i + 1) * 128] = big_a[pl.ds(b * 4 + i, 16, stride=64), :].astype(BF16)

    def send_xa(k, _):
        xy_copy(k, x_as, s_a, xa_ss, xa_rs).start()
        return 0

    lax.fori_loop(1, 16, send_xa, 0)
    s_a[pl.ds(xy, 1)] = x_as[pl.ds(xy, 1)]

    def got_zq(k, _):
        z_arrived(k, z_qr, zq_ss, zq_rs)
        return 0

    lax.fori_loop(1, 16, got_zq, 0)
    big_q[...] = z_qr[...].astype(F32).reshape(640, 128)
    for b in range(16):
        for i in range(2):
            x_qs[b, :, i * 128 : (i + 1) * 128] = big_q[pl.ds(b * 2 + i, 16, stride=40), :].astype(BF16)
            x_qs[b, :, 256 + i * 128 : 256 + (i + 1) * 128] = big_q[
                pl.ds(32 + (b // 4) * 2 + i, 16, stride=40), :
            ].astype(BF16)

    def send_xq(k, _):
        xy_copy(k, x_qs, s_q, xq_ss, xq_rs).start()
        return 0

    lax.fori_loop(1, 16, send_xq, 0)
    s_q[pl.ds(xy, 1)] = x_qs[pl.ds(xy, 1)]

    def sent_factors(k, _):
        factor_copy(k, p_qs, p_qr, pq_ss, pq_rs).wait_send()
        factor_copy(k, p_as, p_ar, pa_ss, pa_rs).wait_send()
        return 0

    lax.fori_loop(1, NT, sent_factors, 0)

    def sent_own(k, _):
        own_copy(k).wait_send()
        return 0

    lax.fori_loop(1, NS, sent_own, 0)

    def sent_z(k, _):
        z_copy(k, z_as, z_ar, za_ss, za_rs).wait_send()
        z_copy(k, z_qs, z_qr, zq_ss, zq_rs).wait_send()
        return 0

    lax.fori_loop(1, 16, sent_z, 0)

    def done_xy(k, _):
        xy_arrived(k, s_a, xa_ss, xa_rs)
        xy_arrived(k, s_q, xq_ss, xq_rs)
        xy_copy(k, x_as, s_a, xa_ss, xa_rs).wait_send()
        xy_copy(k, x_qs, s_q, xq_ss, xq_rs).wait_send()
        return 0

    lax.fori_loop(1, 16, done_xy, 0)


def head_product(head, s_a, s_q, head_own, grad_a, grad_bq, grad_bv, a_v, q_v, v_v, sem):
    copies = []

    def write(src, dst, rows):
        copy = pltpu.make_async_copy(src.at[rows], dst.at[rows], sem.at[len(copies)])
        copy.start()
        copies.append(copy)

    step = H // PIECES
    for p in range(PIECES):
        for r in range(p * step, (p + 1) * step, 256):
            a_v[r : r + 256, :] = mm(head[r : r + 256, :], s_a[...]).astype(BF16)
        write(a_v, grad_a, pl.ds(p * step, step))
        for r in range(p * step, (p + 1) * step, 256):
            q_v[r : r + 256, :] = mm(head[r : r + 256, :], s_q[:, 0:256]).astype(BF16)
        write(q_v, grad_bq, pl.ds(p * step, step))
    v_v[...] = mm(head_own[...], s_q[:, 256:512]).astype(BF16)
    write(v_v, grad_bv, pl.ds(0, H // NS))
    for copy in copies:
        copy.wait()


def shards(acts, grad_q, grad_v, fac_a, fac_bq, fac_bv, seq_tenant, tenant_task, section_layer, task_emb, layer_emb):
    vmem = pl.BlockSpec(memory_space=pltpu.VMEM)
    hbm = pl.BlockSpec(memory_space=pltpu.HBM)
    dma = pltpu.SemaphoreType.DMA
    inputs = (
        acts[0], grad_q[0], grad_v[0], fac_a[0], fac_bq[0], fac_bv[0], seq_tenant,
        tenant_task.reshape(1, TENANTS), section_layer.reshape(1, NS), task_emb, layer_emb,
    )
    s_a, s_q, head, head_own = pl.pallas_call(
        exchange,
        out_shape=(
            pltpu.VMEM((16, 16, 512), BF16),
            pltpu.VMEM((16, 16, 512), BF16),
            pltpu.VMEM((H, NS * NT), BF16),
            pltpu.VMEM((H // NS, NS * NT), BF16),
        ),
        in_specs=[hbm] * len(inputs),
        out_specs=(vmem,) * 4,
        scratch_shapes=[
            pltpu.VMEM((TOK, 8192), BF16),
            pltpu.VMEM((TOK, 8192), BF16),
            pltpu.VMEM((TOK, 1024), BF16),
            pltpu.VMEM((TENANTS, 4096), BF16),
            pltpu.VMEM((TENANTS, 2048), BF16),
            pltpu.VMEM((TENANTS, 256), BF16),
            pltpu.VMEM((TASKS + LAYERS, H), BF16),
            pltpu.VMEM((1, NT), jnp.int32),
            pltpu.VMEM((1, TENANTS), jnp.int32),
            pltpu.VMEM((1, NS), jnp.int32),
            pltpu.VMEM((8, 128), F32),
            pltpu.VMEM((NS, 8, 128), F32),
            pltpu.VMEM((NT * 32, 128), F32),
            pltpu.VMEM((NT * 24, 128), F32),
            pltpu.VMEM((1024, 128), F32),
            pltpu.VMEM((1024, 1024), BF16),
            pltpu.VMEM((512, 2048), BF16),
            pltpu.VMEM((64, 2048), BF16),
            pltpu.VMEM((NT, 32, 128), BF16),
            pltpu.VMEM((NT, 32, 128), BF16),
            pltpu.VMEM((NT, 24, 128), BF16),
            pltpu.VMEM((NT, 24, 128), BF16),
            pltpu.VMEM((16, 64, 128), BF16),
            pltpu.VMEM((16, 64, 128), BF16),
            pltpu.VMEM((16, 40, 128), BF16),
            pltpu.VMEM((16, 40, 128), BF16),
            pltpu.VMEM((16, 16, 512), BF16),
            pltpu.VMEM((16, 16, 512), BF16),
            pltpu.VMEM((1024, 128), F32),
            pltpu.VMEM((640, 128), F32),
            dma((len(inputs),)),
            dma((NS,)), dma((NS,)),
            dma((NT,)), dma((NT,)), dma((NT,)), dma((NT,)),
            dma((16,)), dma((16,)), dma((16,)), dma((16,)),
            dma((16,)), dma((16,)), dma((16,)), dma((16,)),
        ],
        compiler_params=pltpu.CompilerParams(
            collective_id=0, has_side_effects=True, vmem_limit_bytes=36 * 1024 * 1024
        ),
        name="exchange",
    )(*(pltpu.with_memory_space_constraint(a, pltpu.HBM) for a in inputs))
    return pl.pallas_call(
        head_product,
        out_shape=(
            jax.ShapeDtypeStruct((H, 512), BF16),
            jax.ShapeDtypeStruct((H, 256), BF16),
            jax.ShapeDtypeStruct((H // NS, 256), BF16),
        ),
        in_specs=[vmem] * 4,
        out_specs=(hbm,) * 3,
        scratch_shapes=[
            pltpu.VMEM((H, 512), BF16),
            pltpu.VMEM((H, 256), BF16),
            pltpu.VMEM((H // NS, 256), BF16),
            dma((2 * PIECES + 1,)),
        ],
        compiler_params=pltpu.CompilerParams(vmem_limit_bytes=20 * 1024 * 1024),
        name="head_product",
    )(head, s_a.reshape(256, 512), s_q.reshape(256, 512), head_own)


def solution(mesh):
    placed = (
        P("section", "tensor", None),
        P("section", "tensor", None),
        P("section", "tensor", None),
        P("section", None, "tensor"),
        P("section", None, "tensor"),
        P("section", None, "tensor"),
        P("section", None),
        P(),
        P(),
        P(),
        P(),
    )
    return jax.shard_map(
        shards,
        mesh=mesh,
        in_specs=placed,
        out_specs=(
            P(None, ("tensor", "section")),
            P(None, ("tensor", "section")),
            P("section", "tensor"),
        ),
        check_vma=False,
    )
```

```python
import functools
import math

import jax
import jax.numpy as jnp
from jax import lax
from jax.experimental import pallas as pl
from jax.experimental.pallas import tpu as pltpu
from jax.sharding import PartitionSpec as P

MESH = pl.DeviceIdType.MESH
F32, BF16 = jnp.float32, jnp.bfloat16

H = 4096
R = 8
TENANTS = 128
TASKS = 32
LAYERS = 80
TOK = 128
NS, NT = 8, 32
NX, NY, NZL, NZH, NC = 4, 4, 4, 2, 2
HEAD_FIRST = 8
PIECES = 4
SCALE = 2.0 / math.sqrt(TOK * NT * NS)


def mm(a, b):
    return jnp.dot(a, b, preferred_element_type=F32)


def each(first, last, body):
    for k in range(first, last):
        body(k, 0)


def all_in(slots, count, sem):
    some = slots.at[pl.ds(0, count)]
    pltpu.make_async_copy(some, some, sem).wait()


def iota(shape, dim):
    return lax.broadcasted_iota(jnp.int32, shape, dim)


def exchange(
    acts, gq, gv, fa, fq, fv, own, task_of, layer_of, task_emb, layer_emb,
    s_a, s_q, head, head_own, prod_a,
    acts_v, gq_v, gv_v, fa_v, fq_v, fv_v, emb_v, own_v, task_v, layer_v,
    own_s, own_r, gat_a, gat_q, tr, a2, b2, v2,
    p_as, p_ar, p_qs, p_qr, z_as, z_ar, z_qs, z_qr, x_as, x_qs, big_a, big_q,
    load_sem, own_ss, own_rs, pa_ss, pa_rs, pq_ss, pq_rs, za_ss, za_rs, zq_ss, zq_rs, xa_ss, xa_rs, xq_ss, xq_rs,
):
    s, t = lax.axis_index("section"), lax.axis_index("tensor")
    y, zh = lax.div(s, 2), lax.rem(s, 2)
    zl, x, c = lax.div(t, 8), lax.rem(lax.div(t, 2), 4), lax.rem(t, 2)
    zdev = (zl * 2 + zh) * 2 + c
    xy = x * 4 + y

    def around(j, half):
        return half + (j + 1) // 2 * (1 - 2 * (j % 2))

    def tensor_peer(k):
        return lax.rem(t + (k + 1), NT)

    def z_peer(k):
        z = lax.rem(zh * 4 + zl + around(k // 2, 4), 8)
        to_c = lax.rem(c + 1 - (k % 2), 2)
        to_zh = lax.div(z, 4)
        to_zl = z - 4 * to_zh
        return (to_zl * 2 + to_zh) * 2 + to_c, (y * 2 + to_zh, (to_zl * 4 + x) * 2 + to_c)

    def xy_peer(k):
        to_x, to_y = lax.rem(x + around(k // 4, 2), 4), lax.rem(y + around(k % 4, 2), 4)
        return to_x * 4 + to_y, (to_y * 2 + zh, (zl * 4 + to_x) * 2 + c)

    loads = [
        pltpu.make_async_copy(src, dst, load_sem.at[i])
        for i, (src, dst) in enumerate(
            (
                (own, own_v), (fq, fq_v), (fv, fv_v), (fa, fa_v), (gq, gq_v), (gv, gv_v), (acts, acts_v),
                (task_emb, emb_v.at[pl.ds(0, TASKS)]),
                (layer_emb, emb_v.at[pl.ds(TASKS, LAYERS)]),
                (task_of, task_v), (layer_of, layer_v),
            )
        )
    ]
    for load in loads[:4]:
        load.start()

    bar = pltpu.get_barrier_semaphore()

    def greet(section, tensor):
        pl.semaphore_signal(bar, inc=1, device_id=(section, tensor), device_id_type=MESH)

    def greet_tensor(k, _):
        greet(s, tensor_peer(k))
        return 0

    each(0, NT - 1, greet_tensor)

    def greet_z(k, _):
        greet(y * 2 + 1 - zh, ((k // 2) * 4 + x) * 2 + (k % 2))
        return 0

    each(0, NZL * NC, greet_z)

    def greet_xy(k, _):
        greet(lax.rem(y + 1 + (k // 4), NY) * 2 + zh, (zl * 4 + (k % 4)) * 2 + c)
        return 0

    each(0, (NY - 1) * NX, greet_xy)

    def greet_far(k, _):
        greet(lax.rem(y + k, NY) * 2 + 1 - zh, t)
        return 0

    each(1, NY, greet_far)

    for load in loads[4:]:
        load.start()

    loads[0].wait()
    mine = own_v[...]
    hot_t = (iota((TENANTS, NT), 0) == mine).astype(F32).astype(BF16)

    def pick(block):
        return lax.dot_general(hot_t, block, (((0,), (0,)), ((), ())), preferred_element_type=F32)

    loads[1].wait()
    loads[2].wait()
    for i in range(8):
        got = pick(fq_v[:, i * 256 : (i + 1) * 256])
        for h in range(2):
            yy, zz = i // 2, i % 2
            gat_q[pl.ds(zz * 8 + yy * 2 + h, NT, stride=24), :] = got[:, h * 128 : (h + 1) * 128]
    got = pick(fv_v[...])
    for h in range(2):
        gat_q[pl.ds(16 + h, NT, stride=24), :] = got[:, h * 128 : (h + 1) * 128]
    for h in range(6):
        gat_q[pl.ds(18 + h, NT, stride=24), :] = jnp.zeros((NT, 128), F32)
    p_qs[...] = gat_q[...].reshape(NT, 24, 128).astype(BF16)
    p_qr[pl.ds(t, 1)] = p_qs[pl.ds(t, 1)]

    own_s[...] = jnp.broadcast_to(jnp.concatenate([mine.astype(F32), jnp.zeros((1, 96), F32)], axis=1), (8, 128))
    own_r[pl.ds(s, 1)] = own_s[...].reshape(1, 8, 128)

    pl.semaphore_wait(bar, (NT - 1) + NZL * NC + (NY - 1) * NX + NY - 1)

    def factor_copy(k, src, dst, send, recv):
        to = tensor_peer(k)
        return pltpu.make_async_remote_copy(
            src_ref=src.at[to], dst_ref=dst.at[t], send_sem=send, recv_sem=recv,
            device_id=(s, to), device_id_type=MESH,
        )

    def own_copy(k):
        to = lax.rem(s + k, NS)
        return pltpu.make_async_remote_copy(
            src_ref=own_s, dst_ref=own_r.at[s], send_sem=own_ss, recv_sem=own_rs,
            device_id=(to, t), device_id_type=MESH,
        )

    def send_own(k, _):
        own_copy(k).start()
        return 0

    each(1, NS, send_own)

    def send_q(k, _):
        factor_copy(k, p_qs, p_qr, pq_ss, pq_rs).start()
        return 0

    each(0, NT - 1, send_q)

    loads[3].wait()
    for i in range(16):
        got = pick(fa_v[:, i * 256 : (i + 1) * 256])
        for h in range(2):
            n = i * 2 + h
            yy, zz, rr = n // 8, (n // 4) % 2, n % 4
            gat_a[pl.ds(zz * 16 + yy * 4 + rr, NT, stride=32), :] = got[:, h * 128 : (h + 1) * 128]
    p_as[...] = gat_a[...].reshape(NT, 32, 128).astype(BF16)
    p_ar[pl.ds(t, 1)] = p_as[pl.ds(t, 1)]

    def send_a(k, _):
        factor_copy(k, p_as, p_ar, pa_ss, pa_rs).start()
        return 0

    each(0, NT - 1, send_a)

    loads[4].wait()

    def turn_q(i, _):
        zl_, c_, xp = i // 4, (i // 2) % 2, i % 2
        base = pl.multiple_of((i % 2) * 512, 512)
        for xi in range(2):
            tt = (zl_ * 4 + xp * 2 + xi) * 2 + c_
            for h in range(2):
                block = gq_v[:, pl.ds(pl.multiple_of(tt * 256 + h * 128, 128), 128)].astype(F32).T
                for yy in range(2):
                    for zz in range(2):
                        tr[pl.ds(base + zz * 256 + xi * 128 + (2 * h + yy) * 32, 32), :] = block[
                            (yy * 2 + zz) * 32 : (yy * 2 + zz + 1) * 32
                        ]
        for zz in range(2):
            row = pl.multiple_of(((zl_ * 2 + zz) * 2 + c_) * 32 + xp * 16, 16)
            for e in range(16):
                b2[pl.ds(row, 16), e * 128 : (e + 1) * 128] = tr[
                    pl.ds(base + zz * 256 + e, 16, stride=16), :
                ].astype(BF16)
        return 0

    lax.fori_loop(0, 16, turn_q, 0, unroll=2)

    loads[5].wait()
    for zl_ in range(4):
        for h in range(2):
            block = gv_v[:, (zl_ * 2 + h) * 128 : (zl_ * 2 + h + 1) * 128].astype(F32).T
            for xx in range(2):
                for c_ in range(2):
                    to = (zl_ * 2 + c_) * 128 + (2 * h + xx) * 32
                    tr[to : to + 32, :] = block[(xx * 2 + c_) * 32 : (xx * 2 + c_ + 1) * 32]
    for g in range(4):
        for e in range(16):
            v2[g * 16 : (g + 1) * 16, e * 128 : (e + 1) * 128] = tr[pl.ds(g * 256 + e, 16, stride=16), :].astype(BF16)

    loads[6].wait()

    def turn_a(i, _):
        base = pl.multiple_of((i % 4) * 256, 256)
        zl_, x_, c_ = i // 8, (i // 2) % 4, i % 2
        for h in range(2):
            block = acts_v[:, pl.ds(pl.multiple_of(i * 256 + h * 128, 128), 128)].astype(F32).T
            for yy in range(2):
                for zz in range(2):
                    tr[pl.ds(base + zz * 128 + (2 * h + yy) * 32, 32), :] = block[
                        (yy * 2 + zz) * 32 : (yy * 2 + zz + 1) * 32
                    ]
        for zz in range(2):
            row = pl.multiple_of((((zl_ * 2 + zz) * 2 + c_) * 4 + x_) * 16, 16)
            for d in range(8):
                a2[pl.ds(row, 16), d * 128 : (d + 1) * 128] = tr[pl.ds(base + zz * 128 + d, 16, stride=8), :].astype(BF16)
        return 0

    lax.fori_loop(0, 32, turn_a, 0, unroll=4)

    all_in(p_qr, NT - 1, pq_rs)

    places = [(zl_, zz, c_, x_) for zl_ in range(4) for zz in range(2) for c_ in range(2) for x_ in range(4)]
    backq = jnp.zeros((R, TOK), F32)
    fq_rows = jnp.concatenate(
        [p_qr[(zl_ * 4 + x_) * 2 + c_, 0:16, :].astype(F32)[zz * 8 : (zz + 1) * 8] for zl_, zz, c_, x_ in places], axis=0
    )
    fq_t = fq_rows.T.astype(BF16)
    for n in range(8):
        part = mm(fq_t[n * 16 : (n + 1) * 16], b2[:, n * 256 : (n + 1) * 256])
        backq = backq + part[0:8, 0:128] + part[8:16, 128:256]
    fv_rows = jnp.concatenate(
        [p_qr[(zl_ * 4 + x_) * 2 + c_, 16:24, :].astype(F32)[0:2] for zl_ in range(4) for c_ in range(2) for x_ in range(4)],
        axis=0,
    )
    fv_t = jnp.concatenate([fv_rows, jnp.zeros((64, 128), F32)], axis=0).T.astype(BF16)[:, 0:64]
    backv = jnp.zeros((R, TOK), F32)
    for n in range(8):
        part = mm(fv_t[n * 16 : (n + 1) * 16], v2[:, n * 256 : (n + 1) * 256])
        backv = backv + part[0:8, 0:128] + part[8:16, 128:256]
    back_t = jnp.concatenate([backq, backv], axis=0).astype(BF16).astype(F32)
    back = jnp.concatenate([back_t] * 8, axis=0).T
    lane = iota((TOK, 128), 1)
    diag = jnp.concatenate([jnp.where(lane // 16 == d, back, 0.0).astype(BF16) for d in range(8)], axis=0)

    def z_copy(k, src, dst, send, recv):
        q, device = z_peer(k)
        return pltpu.make_async_remote_copy(
            src_ref=src.at[q], dst_ref=dst.at[zdev], send_sem=send, recv_sem=recv,
            device_id=device, device_id_type=MESH,
        )

    for n in range(4):
        z_as[n * 4 : (n + 1) * 4] = (SCALE * mm(a2[n * 256 : (n + 1) * 256, :], diag)).astype(BF16).reshape(4, 64, 128)

    def send_za(k, _):
        z_copy(k, z_as, z_ar, za_ss, za_rs).start()
        return 0

    each(0, 15, send_za)
    z_ar[pl.ds(zdev, 1)] = z_as[pl.ds(zdev, 1)]

    all_in(own_r, NS - 1, own_rs)
    for i in (7, 8, 9, 10):
        loads[i].wait()
    n_seq = NS * NT
    col = iota((1, n_seq), 1)
    col_s = (col // 16 % 4) * 2 + (col // 2) % 2
    col_t = ((col // 4 % 4) * 4 + col // 64) * 2 + col % 2
    owners = jnp.concatenate([own_r[i, 0:1, :] for i in range(NS)], axis=0)
    spread = mm(owners.astype(BF16), (iota((128, n_seq), 0) == col_t).astype(F32).astype(BF16))
    in_section = iota((NS, n_seq), 0) == col_s
    tenant = jnp.sum(jnp.where(in_section, spread, 0.0), axis=0, keepdims=True)
    hot_tenant = (iota((TENANTS, n_seq), 0).astype(F32) == tenant).astype(F32).astype(BF16)
    tasks = jnp.broadcast_to(task_v[...].astype(F32), (8, TENANTS)).astype(BF16)
    task = mm(tasks, hot_tenant)[0:1]
    layers = jnp.broadcast_to(layer_v[...].astype(F32), (NS, NS)).astype(BF16)
    layer = mm(layers, in_section.astype(F32).astype(BF16))[0:1]
    row = iota((TASKS + LAYERS, n_seq), 0).astype(F32)
    hot_head = (row == jnp.where(row < TASKS, task, layer + TASKS)).astype(F32).astype(BF16)

    def head_block(i, _):
        at = pl.multiple_of(i * 256, 256)
        v = lax.dot_general(
            emb_v[:, pl.ds(at, 256)], hot_head, (((0,), (0,)), ((), ())), preferred_element_type=F32
        )
        head[pl.ds(at, 256), :] = (v / (1.0 + jnp.exp(-v))).astype(BF16)
        return 0

    lax.fori_loop(0, HEAD_FIRST, head_block, 0)

    all_in(p_ar, NT - 1, pa_rs)
    fa_rows = jnp.concatenate([p_ar[(zl_ * 4 + x_) * 2 + c_, zz * 16 : (zz + 1) * 16, :] for zl_, zz, c_, x_ in places], axis=0)
    fa_t = fa_rows.astype(F32).T.astype(BF16)
    down_t = jnp.zeros((2 * R, TOK), F32)
    for n in range(4):
        part = mm(fa_t[n * 32 : (n + 1) * 32], a2[:, n * 256 : (n + 1) * 256])
        down_t = down_t + part[0:16, 0:128] + part[16:32, 128:256]
    down_t = down_t.astype(BF16).astype(F32)
    down_q = jnp.concatenate([down_t[0:8]] * 16, axis=0).T
    down_v = jnp.concatenate([down_t[8:16]] * 16, axis=0).T
    diag_q = jnp.concatenate([jnp.where(lane // 8 == e, down_q, 0.0).astype(BF16) for e in range(16)], axis=0)
    diag_v = jnp.concatenate([jnp.where(lane // 8 == e, down_v, 0.0).astype(BF16) for e in range(16)], axis=0)
    grad_v_rows = SCALE * mm(v2[...], diag_v)
    grad_v_rows = grad_v_rows.reshape(8, 8, 128).astype(BF16)
    grad_q_rows = (SCALE * mm(b2[...], diag_q)).astype(BF16).reshape(16, 32, 128)
    for q in range(16):
        z_qs[q, 0:32, :] = grad_q_rows[q]
        z_qs[q, 32:40, :] = grad_v_rows[(q // 4) * 2 + q % 2]

    def send_zq(k, _):
        z_copy(k, z_qs, z_qr, zq_ss, zq_rs).start()
        return 0

    each(0, 15, send_zq)
    z_qr[pl.ds(zdev, 1)] = z_qs[pl.ds(zdev, 1)]

    lax.fori_loop(HEAD_FIRST, H // 256, head_block, 0)
    share = H // NS
    head_own[...] = head[pl.ds(pl.multiple_of(s * share, share), share), :]

    def xy_copy(k, src, dst, send, recv):
        b, device = xy_peer(k)
        return pltpu.make_async_remote_copy(
            src_ref=src.at[b], dst_ref=dst.at[xy], send_sem=send, recv_sem=recv,
            device_id=device, device_id_type=MESH,
        )

    all_in(z_ar, 15, za_rs)
    big_a[...] = z_ar[...].astype(F32).reshape(1024, 128)
    for b in range(16):
        for i in range(4):
            x_as[b, :, i * 128 : (i + 1) * 128] = big_a[pl.ds(b * 4 + i, 16, stride=64), :].astype(BF16)

    def send_xa(k, _):
        xy_copy(k, x_as, s_a, xa_ss, xa_rs).start()
        return 0

    each(0, 15, send_xa)
    s_a[pl.ds(xy, 1)] = x_as[pl.ds(xy, 1)]

    all_in(z_qr, 15, zq_rs)
    big_q[...] = z_qr[...].astype(F32).reshape(640, 128)
    for b in range(16):
        for i in range(2):
            x_qs[b, :, i * 128 : (i + 1) * 128] = big_q[pl.ds(b * 2 + i, 16, stride=40), :].astype(BF16)
            x_qs[b, :, 256 + i * 128 : 256 + (i + 1) * 128] = big_q[
                pl.ds(32 + (b // 4) * 2 + i, 16, stride=40), :
            ].astype(BF16)

    def send_xq(k, _):
        xy_copy(k, x_qs, s_q, xq_ss, xq_rs).start()
        return 0

    each(0, 15, send_xq)
    s_q[pl.ds(xy, 1)] = x_qs[pl.ds(xy, 1)]

    all_in(s_a, 15, xa_rs)

    def product(i, _):
        at = pl.ds(pl.multiple_of(i * 512, 512), 512)
        prod_a[at, :] = mm(head[at, :], s_a[...].reshape(256, 512)).astype(BF16)
        return 0

    lax.fori_loop(0, H // 512, product, 0)

    all_in(p_qs, NT - 1, pq_ss)
    all_in(p_as, NT - 1, pa_ss)

    all_in(own_r, NS - 1, own_ss)

    all_in(z_as, 15, za_ss)
    all_in(z_qs, 15, zq_ss)

    all_in(x_as, 15, xa_ss)
    all_in(x_qs, 15, xq_ss)

    all_in(s_q, 15, xq_rs)


def head_product(head, prod_a, s_q, head_own, grad_a, grad_bq, grad_bv, q_v, v_v, sem):
    copies = []

    def write(src, dst, rows):
        copy = pltpu.make_async_copy(src.at[rows], dst.at[rows], sem.at[len(copies)])
        copy.start()
        copies.append(copy)

    step = H // PIECES
    for p in range(PIECES):
        write(prod_a, grad_a, pl.ds(p * step, step))
    for p in range(PIECES):
        for r in range(p * step, (p + 1) * step, 256):
            q_v[r : r + 256, :] = mm(head[r : r + 256, :], s_q[:, 0:256]).astype(BF16)
        write(q_v, grad_bq, pl.ds(p * step, step))
    v_v[...] = mm(head_own[...], s_q[:, 256:512]).astype(BF16)
    write(v_v, grad_bv, pl.ds(0, H // NS))
    for copy in copies:
        copy.wait()


def shards(acts, grad_q, grad_v, fac_a, fac_bq, fac_bv, seq_tenant, tenant_task, section_layer, task_emb, layer_emb):
    vmem = pl.BlockSpec(memory_space=pltpu.VMEM)
    hbm = pl.BlockSpec(memory_space=pltpu.HBM)
    dma = pltpu.SemaphoreType.DMA
    inputs = (
        acts[0], grad_q[0], grad_v[0], fac_a[0], fac_bq[0], fac_bv[0], seq_tenant,
        tenant_task.reshape(1, TENANTS), section_layer.reshape(1, NS), task_emb, layer_emb,
    )
    _, s_q, head, head_own, prod_a = pl.pallas_call(
        exchange,
        out_shape=(
            pltpu.VMEM((16, 16, 512), BF16),
            pltpu.VMEM((16, 16, 512), BF16),
            pltpu.VMEM((H, NS * NT), BF16),
            pltpu.VMEM((H // NS, NS * NT), BF16),
            pltpu.VMEM((H, 512), BF16),
        ),
        in_specs=[hbm] * len(inputs),
        out_specs=(vmem,) * 5,
        scratch_shapes=[
            pltpu.VMEM((TOK, 8192), BF16),
            pltpu.VMEM((TOK, 8192), BF16),
            pltpu.VMEM((TOK, 1024), BF16),
            pltpu.VMEM((TENANTS, 4096), BF16),
            pltpu.VMEM((TENANTS, 2048), BF16),
            pltpu.VMEM((TENANTS, 256), BF16),
            pltpu.VMEM((TASKS + LAYERS, H), BF16),
            pltpu.VMEM((1, NT), jnp.int32),
            pltpu.VMEM((1, TENANTS), jnp.int32),
            pltpu.VMEM((1, NS), jnp.int32),
            pltpu.VMEM((8, 128), F32),
            pltpu.VMEM((NS, 8, 128), F32),
            pltpu.VMEM((NT * 32, 128), F32),
            pltpu.VMEM((NT * 24, 128), F32),
            pltpu.VMEM((1024, 128), F32),
            pltpu.VMEM((1024, 1024), BF16),
            pltpu.VMEM((512, 2048), BF16),
            pltpu.VMEM((64, 2048), BF16),
            pltpu.VMEM((NT, 32, 128), BF16),
            pltpu.VMEM((NT, 32, 128), BF16),
            pltpu.VMEM((NT, 24, 128), BF16),
            pltpu.VMEM((NT, 24, 128), BF16),
            pltpu.VMEM((16, 64, 128), BF16),
            pltpu.VMEM((16, 64, 128), BF16),
            pltpu.VMEM((16, 40, 128), BF16),
            pltpu.VMEM((16, 40, 128), BF16),
            pltpu.VMEM((16, 16, 512), BF16),
            pltpu.VMEM((16, 16, 512), BF16),
            pltpu.VMEM((1024, 128), F32),
            pltpu.VMEM((640, 128), F32),
            dma((len(inputs),)),
            *([dma] * 14),
        ],
        compiler_params=pltpu.CompilerParams(
            collective_id=0, has_side_effects=True, vmem_limit_bytes=36 * 1024 * 1024
        ),
        name="exchange",
    )(*(pltpu.with_memory_space_constraint(a, pltpu.HBM) for a in inputs))
    return pl.pallas_call(
        head_product,
        out_shape=(
            jax.ShapeDtypeStruct((H, 512), BF16),
            jax.ShapeDtypeStruct((H, 256), BF16),
            jax.ShapeDtypeStruct((H // NS, 256), BF16),
        ),
        in_specs=[vmem] * 4,
        out_specs=(hbm,) * 3,
        scratch_shapes=[
            pltpu.VMEM((H, 256), BF16),
            pltpu.VMEM((H // NS, 256), BF16),
            dma((2 * PIECES + 1,)),
        ],
        compiler_params=pltpu.CompilerParams(vmem_limit_bytes=20 * 1024 * 1024),
        name="head_product",
    )(head, prod_a, s_q.reshape(256, 512), head_own)


def solution(mesh):
    placed = (
        P("section", "tensor", None),
        P("section", "tensor", None),
        P("section", "tensor", None),
        P("section", None, "tensor"),
        P("section", None, "tensor"),
        P("section", None, "tensor"),
        P("section", None),
        P(),
        P(),
        P(),
        P(),
    )
    return jax.shard_map(
        shards,
        mesh=mesh,
        in_specs=placed,
        out_specs=(
            P(None, ("tensor", "section")),
            P(None, ("tensor", "section")),
            P("section", "tensor"),
        ),
        check_vma=False,
    )
```

```python
import functools
import math

import jax
import jax.numpy as jnp
from jax import lax
from jax.experimental import pallas as pl
from jax.experimental.pallas import tpu as pltpu
from jax.sharding import PartitionSpec as P

MESH = pl.DeviceIdType.MESH
F32, BF16 = jnp.float32, jnp.bfloat16

H = 4096
R = 8
TENANTS = 128
TASKS = 32
LAYERS = 80
TOK = 128
NS, NT = 8, 32
NX, NY, NZL, NZH, NC = 4, 4, 4, 2, 2
HEAD_FIRST = 8
PIECES = 4
SCALE = 2.0 / math.sqrt(TOK * NT * NS)


def mm(a, b):
    return jnp.dot(a, b, preferred_element_type=F32)


def each(first, last, body):
    for k in range(first, last):
        body(k, 0)


def all_in(slots, count, sem):
    some = slots.at[pl.ds(0, count)]
    pltpu.make_async_copy(some, some, sem).wait()


def iota(shape, dim):
    return lax.broadcasted_iota(jnp.int32, shape, dim)


def exchange(
    acts, gq, gv, fa, fq, fv, own, task_of, layer_of, task_emb, layer_emb,
    s_a, s_q, head, head_own, prod_a,
    acts_v, gq_v, gv_v, fa_v, fq_v, fv_v, emb_v, own_v, task_v, layer_v,
    own_s, own_r, gat_a, gat_q, tr, a2, b2, v2,
    p_as, p_ar, p_qs, p_qr, p_vs, p_vr, z_as, z_ar, z_qs, z_qr, x_as, x_qs, big_a, big_q,
    load_sem, own_ss, own_rs, pa_ss, pa_rs, pq_ss, pq_rs, pv_ss, pv_rs, za_ss, za_rs, zq_ss, zq_rs, xa_ss, xa_rs, xq_ss, xq_rs,
):
    s, t = lax.axis_index("section"), lax.axis_index("tensor")
    y, zh = lax.div(s, 2), lax.rem(s, 2)
    zl, x, c = lax.div(t, 8), lax.rem(lax.div(t, 2), 4), lax.rem(t, 2)
    zdev = (zl * 2 + zh) * 2 + c
    xy = x * 4 + y

    def around(j, half):
        return half + (j + 1) // 2 * (1 - 2 * (j % 2))

    def tensor_peer(k):
        return lax.rem(t + around(k, NT // 2), NT)

    def z_peer(k):
        z = lax.rem(zh * 4 + zl + around(k // 2, 4), 8)
        to_c = lax.rem(c + 1 - (k % 2), 2)
        to_zh = lax.div(z, 4)
        to_zl = z - 4 * to_zh
        return (to_zl * 2 + to_zh) * 2 + to_c, (y * 2 + to_zh, (to_zl * 4 + x) * 2 + to_c)

    def xy_peer(k):
        to_x, to_y = lax.rem(x + around(k // 4, 2), 4), lax.rem(y + around(k % 4, 2), 4)
        return to_x * 4 + to_y, (to_y * 2 + zh, (zl * 4 + to_x) * 2 + c)

    loads = [
        pltpu.make_async_copy(src, dst, load_sem.at[i])
        for i, (src, dst) in enumerate(
            (
                (own, own_v), (fq, fq_v), (fv, fv_v), (fa, fa_v), (gq, gq_v), (gv, gv_v), (acts, acts_v),
                (task_emb, emb_v.at[pl.ds(0, TASKS)]),
                (layer_emb, emb_v.at[pl.ds(TASKS, LAYERS)]),
                (task_of, task_v), (layer_of, layer_v),
            )
        )
    ]
    for load in loads[:4]:
        load.start()

    bar = pltpu.get_barrier_semaphore()

    def greet(section, tensor):
        pl.semaphore_signal(bar, inc=1, device_id=(section, tensor), device_id_type=MESH)

    def greet_z(k, _):
        greet(y * 2 + 1 - zh, ((k // 2) * 4 + x) * 2 + (k % 2))
        return 0

    each(0, NZL * NC, greet_z)

    def greet_xy(k, _):
        greet(lax.rem(y + 1 + (k // 4), NY) * 2 + zh, (zl * 4 + (k % 4)) * 2 + c)
        return 0

    each(0, (NY - 1) * NX, greet_xy)

    def greet_far(k, _):
        greet(lax.rem(y + k, NY) * 2 + 1 - zh, t)
        return 0

    each(1, NY, greet_far)

    def greet_tensor(k, _):
        greet(s, tensor_peer(k))
        return 0

    each(0, NT - 1, greet_tensor)

    for load in loads[4:]:
        load.start()

    loads[0].wait()
    mine = own_v[...]
    hot_t = (iota((TENANTS, NT), 0) == mine).astype(F32).astype(BF16)

    def pick(block):
        return lax.dot_general(hot_t, block, (((0,), (0,)), ((), ())), preferred_element_type=F32)

    loads[1].wait()
    loads[2].wait()
    for i in range(8):
        got = pick(fq_v[:, i * 256 : (i + 1) * 256])
        for h in range(2):
            yy, zz = i // 2, i % 2
            gat_q[pl.ds(zz * 8 + yy * 2 + h, NT, stride=16), :] = got[:, h * 128 : (h + 1) * 128]
    got = pick(fv_v[...])
    for h in range(2):
        p_vs[:, h, :] = got[:, h * 128 : (h + 1) * 128]
    p_vr[pl.ds(t, 1)] = p_vs[pl.ds(t, 1)]
    p_qs[...] = gat_q[...].reshape(NT, 16, 128).astype(BF16)
    p_qr[pl.ds(t, 1)] = p_qs[pl.ds(t, 1)]

    own_s[...] = jnp.concatenate([mine.astype(F32), jnp.zeros((1, 96), F32)], axis=1)
    own_r[pl.ds(s, 1)] = own_s[...].reshape(1, 1, 128)

    pl.semaphore_wait(bar, (NT - 1) + NZL * NC + (NY - 1) * NX + NY - 1)

    def factor_copy(k, src, dst, send, recv):
        to = tensor_peer(k)
        return pltpu.make_async_remote_copy(
            src_ref=src.at[to], dst_ref=dst.at[t], send_sem=send, recv_sem=recv,
            device_id=(s, to), device_id_type=MESH,
        )

    def own_copy(k):
        to = lax.rem(s + k, NS)
        return pltpu.make_async_remote_copy(
            src_ref=own_s, dst_ref=own_r.at[s], send_sem=own_ss, recv_sem=own_rs,
            device_id=(to, t), device_id_type=MESH,
        )

    def send_own(k, _):
        own_copy(k).start()
        return 0


    def send_q(k, _):
        factor_copy(k, p_vs, p_vr, pv_ss, pv_rs).start()
        factor_copy(k, p_qs, p_qr, pq_ss, pq_rs).start()
        return 0

    each(0, NT - 1, send_q)
    each(1, NS, send_own)

    loads[3].wait()
    for i in range(16):
        got = pick(fa_v[:, i * 256 : (i + 1) * 256])
        for h in range(2):
            n = i * 2 + h
            yy, zz, rr = n // 8, (n // 4) % 2, n % 4
            gat_a[pl.ds(zz * 16 + yy * 4 + rr, NT, stride=32), :] = got[:, h * 128 : (h + 1) * 128]
    p_as[...] = gat_a[...].reshape(NT, 32, 128).astype(BF16)
    p_ar[pl.ds(t, 1)] = p_as[pl.ds(t, 1)]

    def send_a(k, _):
        factor_copy(k, p_as, p_ar, pa_ss, pa_rs).start()
        return 0

    each(0, NT - 1, send_a)

    loads[4].wait()

    def turn_q(i, _):
        zl_, c_, xp = i // 4, (i // 2) % 2, i % 2
        base = pl.multiple_of((i % 2) * 512, 512)
        for xi in range(2):
            tt = (zl_ * 4 + xp * 2 + xi) * 2 + c_
            for h in range(2):
                block = gq_v[:, pl.ds(pl.multiple_of(tt * 256 + h * 128, 128), 128)].astype(F32).T
                for yy in range(2):
                    for zz in range(2):
                        tr[pl.ds(base + zz * 256 + xi * 128 + (2 * h + yy) * 32, 32), :] = block[
                            (yy * 2 + zz) * 32 : (yy * 2 + zz + 1) * 32
                        ]
        for zz in range(2):
            row = pl.multiple_of(((zl_ * 2 + zz) * 2 + c_) * 32 + xp * 16, 16)
            for e in range(16):
                b2[pl.ds(row, 16), e * 128 : (e + 1) * 128] = tr[
                    pl.ds(base + zz * 256 + e, 16, stride=16), :
                ].astype(BF16)
        return 0

    lax.fori_loop(0, 16, turn_q, 0, unroll=2)

    loads[5].wait()
    for zl_ in range(4):
        for h in range(2):
            block = gv_v[:, (zl_ * 2 + h) * 128 : (zl_ * 2 + h + 1) * 128].astype(F32).T
            for xx in range(2):
                for c_ in range(2):
                    to = (zl_ * 2 + c_) * 128 + (2 * h + xx) * 32
                    tr[to : to + 32, :] = block[(xx * 2 + c_) * 32 : (xx * 2 + c_ + 1) * 32]
    for g in range(4):
        for e in range(16):
            v2[g * 16 : (g + 1) * 16, e * 128 : (e + 1) * 128] = tr[pl.ds(g * 256 + e, 16, stride=16), :].astype(BF16)

    loads[6].wait()

    def turn_a(i, _):
        base = pl.multiple_of((i % 4) * 256, 256)
        zl_, x_, c_ = i // 8, (i // 2) % 4, i % 2
        for h in range(2):
            block = acts_v[:, pl.ds(pl.multiple_of(i * 256 + h * 128, 128), 128)].astype(F32).T
            for yy in range(2):
                for zz in range(2):
                    tr[pl.ds(base + zz * 128 + (2 * h + yy) * 32, 32), :] = block[
                        (yy * 2 + zz) * 32 : (yy * 2 + zz + 1) * 32
                    ]
        for zz in range(2):
            row = pl.multiple_of((((zl_ * 2 + zz) * 2 + c_) * 4 + x_) * 16, 16)
            for d in range(8):
                a2[pl.ds(row, 16), d * 128 : (d + 1) * 128] = tr[pl.ds(base + zz * 128 + d, 16, stride=8), :].astype(BF16)
        return 0

    lax.fori_loop(0, 32, turn_a, 0, unroll=4)

    all_in(p_vr, NT - 1, pv_rs)
    all_in(p_qr, NT - 1, pq_rs)

    places = [(zl_, zz, c_, x_) for zl_ in range(4) for zz in range(2) for c_ in range(2) for x_ in range(4)]
    backq = jnp.zeros((R, TOK), F32)
    fq_rows = jnp.concatenate(
        [p_qr[(zl_ * 4 + x_) * 2 + c_, 0:16, :].astype(F32)[zz * 8 : (zz + 1) * 8] for zl_, zz, c_, x_ in places], axis=0
    )
    fq_t = fq_rows.T.astype(BF16)
    for n in range(8):
        part = mm(fq_t[n * 16 : (n + 1) * 16], b2[:, n * 256 : (n + 1) * 256])
        backq = backq + part[0:8, 0:128] + part[8:16, 128:256]
    fv_rows = jnp.concatenate(
        [p_vr[(zl_ * 4 + x_) * 2 + c_] for zl_ in range(4) for c_ in range(2) for x_ in range(4)],
        axis=0,
    )
    fv_t = jnp.concatenate([fv_rows, jnp.zeros((64, 128), F32)], axis=0).T.astype(BF16)[:, 0:64]
    backv = jnp.zeros((R, TOK), F32)
    for n in range(8):
        part = mm(fv_t[n * 16 : (n + 1) * 16], v2[:, n * 256 : (n + 1) * 256])
        backv = backv + part[0:8, 0:128] + part[8:16, 128:256]
    back_t = jnp.concatenate([backq, backv], axis=0).astype(BF16).astype(F32)
    back = jnp.concatenate([back_t] * 8, axis=0).T
    lane = iota((TOK, 128), 1)
    diag = jnp.concatenate([jnp.where(lane // 16 == d, back, 0.0).astype(BF16) for d in range(8)], axis=0)

    def z_copy(k, src, dst, send, recv):
        q, device = z_peer(k)
        return pltpu.make_async_remote_copy(
            src_ref=src.at[q], dst_ref=dst.at[zdev], send_sem=send, recv_sem=recv,
            device_id=device, device_id_type=MESH,
        )

    for n in range(4):
        z_as[n * 4 : (n + 1) * 4] = (SCALE * mm(a2[n * 256 : (n + 1) * 256, :], diag)).astype(BF16).reshape(4, 64, 128)

    def send_za(k, _):
        z_copy(k, z_as, z_ar, za_ss, za_rs).start()
        return 0

    each(0, 15, send_za)
    z_ar[pl.ds(zdev, 1)] = z_as[pl.ds(zdev, 1)]

    all_in(own_r, NS - 1, own_rs)
    for i in (7, 8, 9, 10):
        loads[i].wait()
    n_seq = NS * NT
    col = iota((1, n_seq), 1)
    col_s = (col // 16 % 4) * 2 + (col // 2) % 2
    col_t = ((col // 4 % 4) * 4 + col // 64) * 2 + col % 2
    owners = jnp.concatenate([own_r[i] for i in range(NS)], axis=0)
    spread = mm(owners.astype(BF16), (iota((128, n_seq), 0) == col_t).astype(F32).astype(BF16))
    in_section = iota((NS, n_seq), 0) == col_s
    tenant = jnp.sum(jnp.where(in_section, spread, 0.0), axis=0, keepdims=True)
    hot_tenant = (iota((TENANTS, n_seq), 0).astype(F32) == tenant).astype(F32).astype(BF16)
    tasks = jnp.broadcast_to(task_v[...].astype(F32), (8, TENANTS)).astype(BF16)
    task = mm(tasks, hot_tenant)[0:1]
    layers = jnp.broadcast_to(layer_v[...].astype(F32), (NS, NS)).astype(BF16)
    layer = mm(layers, in_section.astype(F32).astype(BF16))[0:1]
    row = iota((TASKS + LAYERS, n_seq), 0).astype(F32)
    hot_head = (row == jnp.where(row < TASKS, task, layer + TASKS)).astype(F32).astype(BF16)

    def head_block(i, _):
        at = pl.multiple_of(i * 256, 256)
        v = lax.dot_general(
            emb_v[:, pl.ds(at, 256)], hot_head, (((0,), (0,)), ((), ())), preferred_element_type=F32
        )
        head[pl.ds(at, 256), :] = (v / (1.0 + jnp.exp(-v))).astype(BF16)
        return 0

    lax.fori_loop(0, HEAD_FIRST, head_block, 0)

    all_in(p_ar, NT - 1, pa_rs)
    fa_rows = jnp.concatenate([p_ar[(zl_ * 4 + x_) * 2 + c_, zz * 16 : (zz + 1) * 16, :] for zl_, zz, c_, x_ in places], axis=0)
    fa_t = fa_rows.astype(F32).T.astype(BF16)
    down_t = jnp.zeros((2 * R, TOK), F32)
    for n in range(4):
        part = mm(fa_t[n * 32 : (n + 1) * 32], a2[:, n * 256 : (n + 1) * 256])
        down_t = down_t + part[0:16, 0:128] + part[16:32, 128:256]
    down_t = down_t.astype(BF16).astype(F32)
    down_q = jnp.concatenate([down_t[0:8]] * 16, axis=0).T
    down_v = jnp.concatenate([down_t[8:16]] * 16, axis=0).T
    diag_q = jnp.concatenate([jnp.where(lane // 8 == e, down_q, 0.0).astype(BF16) for e in range(16)], axis=0)
    diag_v = jnp.concatenate([jnp.where(lane // 8 == e, down_v, 0.0).astype(BF16) for e in range(16)], axis=0)
    grad_v_rows = SCALE * mm(v2[...], diag_v)
    grad_v_rows = grad_v_rows.reshape(8, 8, 128).astype(BF16)
    grad_q_rows = (SCALE * mm(b2[...], diag_q)).astype(BF16).reshape(16, 32, 128)
    for q in range(16):
        z_qs[q, 0:32, :] = grad_q_rows[q]
        z_qs[q, 32:40, :] = grad_v_rows[(q // 4) * 2 + q % 2]

    def send_zq(k, _):
        z_copy(k, z_qs, z_qr, zq_ss, zq_rs).start()
        return 0

    each(0, 15, send_zq)
    z_qr[pl.ds(zdev, 1)] = z_qs[pl.ds(zdev, 1)]

    lax.fori_loop(HEAD_FIRST, H // 256, head_block, 0)
    share = H // NS
    head_own[...] = head[pl.ds(pl.multiple_of(s * share, share), share), :]

    def xy_copy(k, src, dst, send, recv):
        b, device = xy_peer(k)
        return pltpu.make_async_remote_copy(
            src_ref=src.at[b], dst_ref=dst.at[xy], send_sem=send, recv_sem=recv,
            device_id=device, device_id_type=MESH,
        )

    all_in(z_ar, 15, za_rs)
    big_a[...] = z_ar[...].astype(F32).reshape(1024, 128)
    for b in range(16):
        for i in range(4):
            x_as[b, :, i * 128 : (i + 1) * 128] = big_a[pl.ds(b * 4 + i, 16, stride=64), :].astype(BF16)

    def send_xa(k, _):
        xy_copy(k, x_as, s_a, xa_ss, xa_rs).start()
        return 0

    each(0, 15, send_xa)
    s_a[pl.ds(xy, 1)] = x_as[pl.ds(xy, 1)]

    all_in(z_qr, 15, zq_rs)
    big_q[...] = z_qr[...].astype(F32).reshape(640, 128)
    for b in range(16):
        for i in range(2):
            x_qs[b, :, i * 128 : (i + 1) * 128] = big_q[pl.ds(b * 2 + i, 16, stride=40), :].astype(BF16)
            x_qs[b, :, 256 + i * 128 : 256 + (i + 1) * 128] = big_q[
                pl.ds(32 + (b // 4) * 2 + i, 16, stride=40), :
            ].astype(BF16)

    def send_xq(k, _):
        xy_copy(k, x_qs, s_q, xq_ss, xq_rs).start()
        return 0

    each(0, 15, send_xq)
    s_q[pl.ds(xy, 1)] = x_qs[pl.ds(xy, 1)]

    all_in(s_a, 15, xa_rs)

    def product(i, _):
        at = pl.ds(pl.multiple_of(i * 512, 512), 512)
        prod_a[at, :] = mm(head[at, :], s_a[...].reshape(256, 512)).astype(BF16)
        return 0

    lax.fori_loop(0, H // 512, product, 0)

    all_in(p_vs, NT - 1, pv_ss)
    all_in(p_qs, NT - 1, pq_ss)
    all_in(p_as, NT - 1, pa_ss)

    all_in(own_r, NS - 1, own_ss)

    all_in(z_as, 15, za_ss)
    all_in(z_qs, 15, zq_ss)

    all_in(x_as, 15, xa_ss)
    all_in(x_qs, 15, xq_ss)

    all_in(s_q, 15, xq_rs)


def head_product(head, prod_a, s_q, head_own, grad_a, grad_bq, grad_bv, q_v, v_v, sem):
    copies = []

    def write(src, dst, rows):
        copy = pltpu.make_async_copy(src.at[rows], dst.at[rows], sem.at[len(copies)])
        copy.start()
        copies.append(copy)

    step = H // PIECES
    for p in range(PIECES):
        write(prod_a, grad_a, pl.ds(p * step, step))
    for p in range(PIECES):
        for r in range(p * step, (p + 1) * step, 256):
            q_v[r : r + 256, :] = mm(head[r : r + 256, :], s_q[:, 0:256]).astype(BF16)
        write(q_v, grad_bq, pl.ds(p * step, step))
    v_v[...] = mm(head_own[...], s_q[:, 256:512]).astype(BF16)
    write(v_v, grad_bv, pl.ds(0, H // NS))
    for copy in copies:
        copy.wait()


def shards(acts, grad_q, grad_v, fac_a, fac_bq, fac_bv, seq_tenant, tenant_task, section_layer, task_emb, layer_emb):
    vmem = pl.BlockSpec(memory_space=pltpu.VMEM)
    hbm = pl.BlockSpec(memory_space=pltpu.HBM)
    dma = pltpu.SemaphoreType.DMA
    inputs = (
        acts[0], grad_q[0], grad_v[0], fac_a[0], fac_bq[0], fac_bv[0], seq_tenant,
        tenant_task.reshape(1, TENANTS), section_layer.reshape(1, NS), task_emb, layer_emb,
    )
    _, s_q, head, head_own, prod_a = pl.pallas_call(
        exchange,
        out_shape=(
            pltpu.VMEM((16, 16, 512), BF16),
            pltpu.VMEM((16, 16, 512), BF16),
            pltpu.VMEM((H, NS * NT), BF16),
            pltpu.VMEM((H // NS, NS * NT), BF16),
            pltpu.VMEM((H, 512), BF16),
        ),
        in_specs=[hbm] * len(inputs),
        out_specs=(vmem,) * 5,
        scratch_shapes=[
            pltpu.VMEM((TOK, 8192), BF16),
            pltpu.VMEM((TOK, 8192), BF16),
            pltpu.VMEM((TOK, 1024), BF16),
            pltpu.VMEM((TENANTS, 4096), BF16),
            pltpu.VMEM((TENANTS, 2048), BF16),
            pltpu.VMEM((TENANTS, 256), BF16),
            pltpu.VMEM((TASKS + LAYERS, H), BF16),
            pltpu.VMEM((1, NT), jnp.int32),
            pltpu.VMEM((1, TENANTS), jnp.int32),
            pltpu.VMEM((1, NS), jnp.int32),
            pltpu.VMEM((1, 128), F32),
            pltpu.VMEM((NS, 1, 128), F32),
            pltpu.VMEM((NT * 32, 128), F32),
            pltpu.VMEM((NT * 16, 128), F32),
            pltpu.VMEM((1024, 128), F32),
            pltpu.VMEM((1024, 1024), BF16),
            pltpu.VMEM((512, 2048), BF16),
            pltpu.VMEM((64, 2048), BF16),
            pltpu.VMEM((NT, 32, 128), BF16),
            pltpu.VMEM((NT, 32, 128), BF16),
            pltpu.VMEM((NT, 16, 128), BF16),
            pltpu.VMEM((NT, 16, 128), BF16),
            pltpu.VMEM((NT, 2, 128), F32),
            pltpu.VMEM((NT, 2, 128), F32),
            pltpu.VMEM((16, 64, 128), BF16),
            pltpu.VMEM((16, 64, 128), BF16),
            pltpu.VMEM((16, 40, 128), BF16),
            pltpu.VMEM((16, 40, 128), BF16),
            pltpu.VMEM((16, 16, 512), BF16),
            pltpu.VMEM((16, 16, 512), BF16),
            pltpu.VMEM((1024, 128), F32),
            pltpu.VMEM((640, 128), F32),
            dma((len(inputs),)),
            *([dma] * 16),
        ],
        compiler_params=pltpu.CompilerParams(
            collective_id=0, has_side_effects=True, vmem_limit_bytes=36 * 1024 * 1024
        ),
        name="exchange",
    )(*(pltpu.with_memory_space_constraint(a, pltpu.HBM) for a in inputs))
    return pl.pallas_call(
        head_product,
        out_shape=(
            jax.ShapeDtypeStruct((H, 512), BF16),
            jax.ShapeDtypeStruct((H, 256), BF16),
            jax.ShapeDtypeStruct((H // NS, 256), BF16),
        ),
        in_specs=[vmem] * 4,
        out_specs=(hbm,) * 3,
        scratch_shapes=[
            pltpu.VMEM((H, 256), BF16),
            pltpu.VMEM((H // NS, 256), BF16),
            dma((2 * PIECES + 1,)),
        ],
        compiler_params=pltpu.CompilerParams(vmem_limit_bytes=20 * 1024 * 1024),
        name="head_product",
    )(head, prod_a, s_q.reshape(256, 512), head_own)


def solution(mesh):
    placed = (
        P("section", "tensor", None),
        P("section", "tensor", None),
        P("section", "tensor", None),
        P("section", None, "tensor"),
        P("section", None, "tensor"),
        P("section", None, "tensor"),
        P("section", None),
        P(),
        P(),
        P(),
        P(),
    )
    return jax.shard_map(
        shards,
        mesh=mesh,
        in_specs=placed,
        out_specs=(
            P(None, ("tensor", "section")),
            P(None, ("tensor", "section")),
            P("section", "tensor"),
        ),
        check_vma=False,
    )
```

```python
import functools
import math

import jax
import jax.numpy as jnp
from jax import lax
from jax.experimental import pallas as pl
from jax.experimental.pallas import tpu as pltpu
from jax.sharding import PartitionSpec as P

MESH = pl.DeviceIdType.MESH
F32, BF16 = jnp.float32, jnp.bfloat16

H = 4096
R = 8
TENANTS = 128
TASKS = 32
LAYERS = 80
TOK = 128
NS, NT = 8, 32
NX, NY, NZL, NZH, NC = 4, 4, 4, 2, 2
HEAD_FIRST = 8
PIECES = 4
SCALE = 2.0 / math.sqrt(TOK * NT * NS)


def mm(a, b):
    return jnp.dot(a, b, preferred_element_type=F32)


def each(first, last, body):
    for k in range(first, last):
        body(k, 0)


def all_in(slots, count, sem):
    some = slots.at[pl.ds(0, count)]
    pltpu.make_async_copy(some, some, sem).wait()


def iota(shape, dim):
    return lax.broadcasted_iota(jnp.int32, shape, dim)


def exchange(
    acts, gq, gv, fa, fq, fv, own, task_of, layer_of, task_emb, layer_emb,
    s_a, s_q, head, head_own, prod_a,
    acts_v, gq_v, gv_v, fa_v, fq_v, fv_v, emb_v, own_v, task_v, layer_v,
    own_s, own_r, gat_a, gat_q, tr, a2, b2, v2,
    p_as, p_ar, p_qs, p_qr, p_vs, p_vr, z_as, z_ar, z_qs, z_qr, x_as, x_qs, big_a, big_q,
    load_sem, own_ss, own_rs, pa_ss, pa_rs, pq_ss, pq_rs, pv_ss, pv_rs, za_ss, za_rs, zq_ss, zq_rs, xa_ss, xa_rs, xq_ss, xq_rs,
):
    s, t = lax.axis_index("section"), lax.axis_index("tensor")
    y, zh = lax.div(s, 2), lax.rem(s, 2)
    zl, x, c = lax.div(t, 8), lax.rem(lax.div(t, 2), 4), lax.rem(t, 2)
    zdev = (zl * 2 + zh) * 2 + c
    xy = x * 4 + y

    def around(j, half):
        return half + (j + 1) // 2 * (1 - 2 * (j % 2))

    def tensor_peer(k):
        return lax.rem(t + around(k, NT // 2), NT)

    def z_peer(k):
        z = lax.rem(zh * 4 + zl + around(k % 8, 4), 8)
        to_c = lax.rem(c + 1 - k // 8, 2)
        to_zh = lax.div(z, 4)
        to_zl = z - 4 * to_zh
        return (to_zl * 2 + to_zh) * 2 + to_c, (y * 2 + to_zh, (to_zl * 4 + x) * 2 + to_c)

    def xy_peer(k):
        to_x, to_y = lax.rem(x + around(k // 4, 2), 4), lax.rem(y + around(k % 4, 2), 4)
        return to_x * 4 + to_y, (to_y * 2 + zh, (zl * 4 + to_x) * 2 + c)

    loads = [
        pltpu.make_async_copy(src, dst, load_sem.at[i])
        for i, (src, dst) in enumerate(
            (
                (own, own_v), (fq, fq_v), (fv, fv_v), (fa, fa_v), (gq, gq_v), (gv, gv_v), (acts, acts_v),
                (task_emb, emb_v.at[pl.ds(0, TASKS)]),
                (layer_emb, emb_v.at[pl.ds(TASKS, LAYERS)]),
                (task_of, task_v), (layer_of, layer_v),
            )
        )
    ]
    for load in loads[:4]:
        load.start()

    bar = pltpu.get_barrier_semaphore()

    def greet(section, tensor):
        pl.semaphore_signal(bar, inc=1, device_id=(section, tensor), device_id_type=MESH)

    def greet_z(k, _):
        greet(y * 2 + 1 - zh, ((k // 2) * 4 + x) * 2 + (k % 2))
        return 0

    each(0, NZL * NC, greet_z)

    def greet_xy(k, _):
        greet(lax.rem(y + 1 + (k // 4), NY) * 2 + zh, (zl * 4 + (k % 4)) * 2 + c)
        return 0

    each(0, (NY - 1) * NX, greet_xy)

    def greet_far(k, _):
        greet(lax.rem(y + k, NY) * 2 + 1 - zh, t)
        return 0

    each(1, NY, greet_far)

    def greet_tensor(k, _):
        greet(s, tensor_peer(k))
        return 0

    each(0, NT - 1, greet_tensor)

    for load in loads[4:]:
        load.start()

    loads[0].wait()
    mine = own_v[...]
    hot_t = (iota((TENANTS, NT), 0) == mine).astype(F32).astype(BF16)

    def pick(block):
        return lax.dot_general(hot_t, block, (((0,), (0,)), ((), ())), preferred_element_type=F32)

    loads[1].wait()
    loads[2].wait()
    for i in range(8):
        got = pick(fq_v[:, i * 256 : (i + 1) * 256])
        for h in range(2):
            yy, zz = i // 2, i % 2
            gat_q[pl.ds(zz * 8 + yy * 2 + h, NT, stride=16), :] = got[:, h * 128 : (h + 1) * 128]
    got = pick(fv_v[...])
    for h in range(2):
        p_vs[:, h, :] = got[:, h * 128 : (h + 1) * 128]
    p_vr[pl.ds(t, 1)] = p_vs[pl.ds(t, 1)]
    p_qs[...] = gat_q[...].reshape(NT, 16, 128).astype(BF16)
    p_qr[pl.ds(t, 1)] = p_qs[pl.ds(t, 1)]

    own_s[...] = jnp.concatenate([mine.astype(F32), jnp.zeros((1, 96), F32)], axis=1)
    own_r[pl.ds(s, 1)] = own_s[...].reshape(1, 1, 128)

    pl.semaphore_wait(bar, (NT - 1) + NZL * NC + (NY - 1) * NX + NY - 1)

    def factor_copy(k, src, dst, send, recv):
        to = tensor_peer(k)
        return pltpu.make_async_remote_copy(
            src_ref=src.at[to], dst_ref=dst.at[t], send_sem=send, recv_sem=recv,
            device_id=(s, to), device_id_type=MESH,
        )

    def own_copy(k):
        to = lax.rem(s + k, NS)
        return pltpu.make_async_remote_copy(
            src_ref=own_s, dst_ref=own_r.at[s], send_sem=own_ss, recv_sem=own_rs,
            device_id=(to, t), device_id_type=MESH,
        )

    def send_own(k, _):
        own_copy(k).start()
        return 0


    def send_q(k, _):
        factor_copy(k, p_vs, p_vr, pv_ss, pv_rs).start()
        factor_copy(k, p_qs, p_qr, pq_ss, pq_rs).start()
        return 0

    each(0, NT - 1, send_q)

    loads[3].wait()
    for i in range(16):
        got = pick(fa_v[:, i * 256 : (i + 1) * 256])
        for h in range(2):
            n = i * 2 + h
            yy, zz, rr = n // 8, (n // 4) % 2, n % 4
            gat_a[pl.ds(zz * 16 + yy * 4 + rr, NT, stride=32), :] = got[:, h * 128 : (h + 1) * 128]
    p_as[...] = gat_a[...].reshape(NT, 32, 128).astype(BF16)
    p_ar[pl.ds(t, 1)] = p_as[pl.ds(t, 1)]

    def send_a(k, _):
        factor_copy(k, p_as, p_ar, pa_ss, pa_rs).start()
        return 0

    each(0, NT - 1, send_a)
    each(1, NS, send_own)

    loads[4].wait()

    def turn_q(i, _):
        zl_, c_, xp = i // 4, (i // 2) % 2, i % 2
        base = pl.multiple_of((i % 2) * 512, 512)
        for xi in range(2):
            tt = (zl_ * 4 + xp * 2 + xi) * 2 + c_
            for h in range(2):
                block = gq_v[:, pl.ds(pl.multiple_of(tt * 256 + h * 128, 128), 128)].astype(F32).T
                for yy in range(2):
                    for zz in range(2):
                        tr[pl.ds(base + zz * 256 + xi * 128 + (2 * h + yy) * 32, 32), :] = block[
                            (yy * 2 + zz) * 32 : (yy * 2 + zz + 1) * 32
                        ]
        for zz in range(2):
            row = pl.multiple_of(((zl_ * 2 + zz) * 2 + c_) * 32 + xp * 16, 16)
            for e in range(16):
                b2[pl.ds(row, 16), e * 128 : (e + 1) * 128] = tr[
                    pl.ds(base + zz * 256 + e, 16, stride=16), :
                ].astype(BF16)
        return 0

    lax.fori_loop(0, 16, turn_q, 0, unroll=2)

    loads[5].wait()
    for zl_ in range(4):
        for h in range(2):
            block = gv_v[:, (zl_ * 2 + h) * 128 : (zl_ * 2 + h + 1) * 128].astype(F32).T
            for xx in range(2):
                for c_ in range(2):
                    to = (zl_ * 2 + c_) * 128 + (2 * h + xx) * 32
                    tr[to : to + 32, :] = block[(xx * 2 + c_) * 32 : (xx * 2 + c_ + 1) * 32]
    for g in range(4):
        for e in range(16):
            v2[g * 16 : (g + 1) * 16, e * 128 : (e + 1) * 128] = tr[pl.ds(g * 256 + e, 16, stride=16), :].astype(BF16)

    loads[6].wait()

    def turn_a(i, _):
        base = pl.multiple_of((i % 4) * 256, 256)
        zl_, x_, c_ = i // 8, (i // 2) % 4, i % 2
        for h in range(2):
            block = acts_v[:, pl.ds(pl.multiple_of(i * 256 + h * 128, 128), 128)].astype(F32).T
            for yy in range(2):
                for zz in range(2):
                    tr[pl.ds(base + zz * 128 + (2 * h + yy) * 32, 32), :] = block[
                        (yy * 2 + zz) * 32 : (yy * 2 + zz + 1) * 32
                    ]
        for zz in range(2):
            row = pl.multiple_of((((zl_ * 2 + zz) * 2 + c_) * 4 + x_) * 16, 16)
            for d in range(8):
                a2[pl.ds(row, 16), d * 128 : (d + 1) * 128] = tr[pl.ds(base + zz * 128 + d, 16, stride=8), :].astype(BF16)
        return 0

    lax.fori_loop(0, 32, turn_a, 0, unroll=4)

    all_in(p_vr, NT - 1, pv_rs)
    all_in(p_qr, NT - 1, pq_rs)

    places = [(zl_, zz, c_, x_) for zl_ in range(4) for zz in range(2) for c_ in range(2) for x_ in range(4)]
    backq = jnp.zeros((R, TOK), F32)
    fq_rows = jnp.concatenate(
        [p_qr[(zl_ * 4 + x_) * 2 + c_, 0:16, :].astype(F32)[zz * 8 : (zz + 1) * 8] for zl_, zz, c_, x_ in places], axis=0
    )
    fq_t = fq_rows.T.astype(BF16)
    for n in range(8):
        part = mm(fq_t[n * 16 : (n + 1) * 16], b2[:, n * 256 : (n + 1) * 256])
        backq = backq + part[0:8, 0:128] + part[8:16, 128:256]
    fv_rows = jnp.concatenate(
        [p_vr[(zl_ * 4 + x_) * 2 + c_] for zl_ in range(4) for c_ in range(2) for x_ in range(4)],
        axis=0,
    )
    fv_t = jnp.concatenate([fv_rows, jnp.zeros((64, 128), F32)], axis=0).T.astype(BF16)[:, 0:64]
    backv = jnp.zeros((R, TOK), F32)
    for n in range(8):
        part = mm(fv_t[n * 16 : (n + 1) * 16], v2[:, n * 256 : (n + 1) * 256])
        backv = backv + part[0:8, 0:128] + part[8:16, 128:256]
    back_t = jnp.concatenate([backq, backv], axis=0).astype(BF16).astype(F32)
    back = jnp.concatenate([back_t] * 8, axis=0).T
    lane = iota((TOK, 128), 1)
    diag = jnp.concatenate([jnp.where(lane // 16 == d, back, 0.0).astype(BF16) for d in range(8)], axis=0)

    def z_copy(k, src, dst, send, recv):
        q, device = z_peer(k)
        return pltpu.make_async_remote_copy(
            src_ref=src.at[q], dst_ref=dst.at[zdev], send_sem=send, recv_sem=recv,
            device_id=device, device_id_type=MESH,
        )

    for n in range(4):
        z_as[n * 4 : (n + 1) * 4] = (SCALE * mm(a2[n * 256 : (n + 1) * 256, :], diag)).astype(BF16).reshape(4, 64, 128)

    def send_za(k, _):
        z_copy(k, z_as, z_ar, za_ss, za_rs).start()
        return 0

    each(0, 15, send_za)
    z_ar[pl.ds(zdev, 1)] = z_as[pl.ds(zdev, 1)]

    all_in(own_r, NS - 1, own_rs)
    for i in (7, 8, 9, 10):
        loads[i].wait()
    n_seq = NS * NT
    col = iota((1, n_seq), 1)
    col_s = (col // 16 % 4) * 2 + (col // 2) % 2
    col_t = ((col // 4 % 4) * 4 + col // 64) * 2 + col % 2
    owners = jnp.concatenate([own_r[i] for i in range(NS)], axis=0)
    spread = mm(owners.astype(BF16), (iota((128, n_seq), 0) == col_t).astype(F32).astype(BF16))
    in_section = iota((NS, n_seq), 0) == col_s
    tenant = jnp.sum(jnp.where(in_section, spread, 0.0), axis=0, keepdims=True)
    hot_tenant = (iota((TENANTS, n_seq), 0).astype(F32) == tenant).astype(F32).astype(BF16)
    tasks = jnp.broadcast_to(task_v[...].astype(F32), (8, TENANTS)).astype(BF16)
    task = mm(tasks, hot_tenant)[0:1]
    layers = jnp.broadcast_to(layer_v[...].astype(F32), (NS, NS)).astype(BF16)
    layer = mm(layers, in_section.astype(F32).astype(BF16))[0:1]
    row = iota((TASKS + LAYERS, n_seq), 0).astype(F32)
    hot_head = (row == jnp.where(row < TASKS, task, layer + TASKS)).astype(F32).astype(BF16)

    def head_block(i, _):
        at = pl.multiple_of(i * 256, 256)
        v = lax.dot_general(
            emb_v[:, pl.ds(at, 256)], hot_head, (((0,), (0,)), ((), ())), preferred_element_type=F32
        )
        head[pl.ds(at, 256), :] = (v / (1.0 + jnp.exp(-v))).astype(BF16)
        return 0

    lax.fori_loop(0, HEAD_FIRST, head_block, 0)

    all_in(p_ar, NT - 1, pa_rs)
    fa_rows = jnp.concatenate([p_ar[(zl_ * 4 + x_) * 2 + c_, zz * 16 : (zz + 1) * 16, :] for zl_, zz, c_, x_ in places], axis=0)
    fa_t = fa_rows.astype(F32).T.astype(BF16)
    down_t = jnp.zeros((2 * R, TOK), F32)
    for n in range(4):
        part = mm(fa_t[n * 32 : (n + 1) * 32], a2[:, n * 256 : (n + 1) * 256])
        down_t = down_t + part[0:16, 0:128] + part[16:32, 128:256]
    down_t = down_t.astype(BF16).astype(F32)
    down_q = jnp.concatenate([down_t[0:8]] * 16, axis=0).T
    down_v = jnp.concatenate([down_t[8:16]] * 16, axis=0).T
    diag_q = jnp.concatenate([jnp.where(lane // 8 == e, down_q, 0.0).astype(BF16) for e in range(16)], axis=0)
    diag_v = jnp.concatenate([jnp.where(lane // 8 == e, down_v, 0.0).astype(BF16) for e in range(16)], axis=0)
    grad_v_rows = SCALE * mm(v2[...], diag_v)
    grad_v_rows = jnp.concatenate([grad_v_rows.reshape(8, 8, 128), jnp.zeros((8, 8, 128), F32)], axis=1).astype(BF16)
    grad_q_rows = (SCALE * mm(b2[...], diag_q)).astype(BF16).reshape(16, 32, 128)
    for q in range(16):
        z_qs[q, 0:32, :] = grad_q_rows[q]
        z_qs[q, 32:48, :] = grad_v_rows[(q // 4) * 2 + q % 2]

    def send_zq(k, _):
        z_copy(k, z_qs, z_qr, zq_ss, zq_rs).start()
        return 0

    each(0, 15, send_zq)
    z_qr[pl.ds(zdev, 1)] = z_qs[pl.ds(zdev, 1)]

    lax.fori_loop(HEAD_FIRST, H // 256, head_block, 0)
    share = H // NS
    head_own[...] = head[pl.ds(pl.multiple_of(s * share, share), share), :]

    def xy_copy(k, src, dst, send, recv):
        b, device = xy_peer(k)
        return pltpu.make_async_remote_copy(
            src_ref=src.at[b], dst_ref=dst.at[xy], send_sem=send, recv_sem=recv,
            device_id=device, device_id_type=MESH,
        )

    all_in(z_ar, 15, za_rs)
    big_a[...] = z_ar[...].astype(F32).reshape(1024, 128)
    for b in range(16):
        for i in range(4):
            x_as[b, :, i * 128 : (i + 1) * 128] = big_a[pl.ds(b * 4 + i, 16, stride=64), :].astype(BF16)

    def send_xa(k, _):
        xy_copy(k, x_as, s_a, xa_ss, xa_rs).start()
        return 0

    each(0, 15, send_xa)
    s_a[pl.ds(xy, 1)] = x_as[pl.ds(xy, 1)]

    all_in(z_qr, 15, zq_rs)
    big_q[...] = z_qr[...].astype(F32).reshape(768, 128)
    for b in range(16):
        for i in range(2):
            x_qs[b, :, i * 128 : (i + 1) * 128] = big_q[pl.ds(b * 2 + i, 16, stride=48), :].astype(BF16)
            x_qs[b, :, 256 + i * 128 : 256 + (i + 1) * 128] = big_q[
                pl.ds(32 + (b // 4) * 2 + i, 16, stride=48), :
            ].astype(BF16)

    def send_xq(k, _):
        xy_copy(k, x_qs, s_q, xq_ss, xq_rs).start()
        return 0

    each(0, 15, send_xq)
    s_q[pl.ds(xy, 1)] = x_qs[pl.ds(xy, 1)]

    all_in(s_a, 15, xa_rs)

    def product(i, _):
        at = pl.ds(pl.multiple_of(i * 512, 512), 512)
        prod_a[at, :] = mm(head[at, :], s_a[...].reshape(256, 512)).astype(BF16)
        return 0

    lax.fori_loop(0, H // 512, product, 0)

    all_in(p_vs, NT - 1, pv_ss)
    all_in(p_qs, NT - 1, pq_ss)
    all_in(p_as, NT - 1, pa_ss)

    all_in(own_r, NS - 1, own_ss)

    all_in(z_as, 15, za_ss)
    all_in(z_qs, 15, zq_ss)

    all_in(x_as, 15, xa_ss)
    all_in(x_qs, 15, xq_ss)

    all_in(s_q, 15, xq_rs)


def head_product(head, prod_a, s_q, head_own, grad_a, grad_bq, grad_bv, q_v, v_v, sem):
    copies = []

    def write(src, dst, rows):
        copy = pltpu.make_async_copy(src.at[rows], dst.at[rows], sem.at[len(copies)])
        copy.start()
        copies.append(copy)

    step = H // PIECES
    for p in range(PIECES):
        write(prod_a, grad_a, pl.ds(p * step, step))
    for p in range(PIECES):
        for r in range(p * step, (p + 1) * step, 256):
            q_v[r : r + 256, :] = mm(head[r : r + 256, :], s_q[:, 0:256]).astype(BF16)
        write(q_v, grad_bq, pl.ds(p * step, step))
    v_v[...] = mm(head_own[...], s_q[:, 256:512]).astype(BF16)
    write(v_v, grad_bv, pl.ds(0, H // NS))
    for copy in copies:
        copy.wait()


def shards(acts, grad_q, grad_v, fac_a, fac_bq, fac_bv, seq_tenant, tenant_task, section_layer, task_emb, layer_emb):
    vmem = pl.BlockSpec(memory_space=pltpu.VMEM)
    hbm = pl.BlockSpec(memory_space=pltpu.HBM)
    dma = pltpu.SemaphoreType.DMA
    inputs = (
        acts[0], grad_q[0], grad_v[0], fac_a[0], fac_bq[0], fac_bv[0], seq_tenant,
        tenant_task.reshape(1, TENANTS), section_layer.reshape(1, NS), task_emb, layer_emb,
    )
    _, s_q, head, head_own, prod_a = pl.pallas_call(
        exchange,
        out_shape=(
            pltpu.VMEM((16, 16, 512), BF16),
            pltpu.VMEM((16, 16, 512), BF16),
            pltpu.VMEM((H, NS * NT), BF16),
            pltpu.VMEM((H // NS, NS * NT), BF16),
            pltpu.VMEM((H, 512), BF16),
        ),
        in_specs=[hbm] * len(inputs),
        out_specs=(vmem,) * 5,
        scratch_shapes=[
            pltpu.VMEM((TOK, 8192), BF16),
            pltpu.VMEM((TOK, 8192), BF16),
            pltpu.VMEM((TOK, 1024), BF16),
            pltpu.VMEM((TENANTS, 4096), BF16),
            pltpu.VMEM((TENANTS, 2048), BF16),
            pltpu.VMEM((TENANTS, 256), BF16),
            pltpu.VMEM((TASKS + LAYERS, H), BF16),
            pltpu.VMEM((1, NT), jnp.int32),
            pltpu.VMEM((1, TENANTS), jnp.int32),
            pltpu.VMEM((1, NS), jnp.int32),
            pltpu.VMEM((1, 128), F32),
            pltpu.VMEM((NS, 1, 128), F32),
            pltpu.VMEM((NT * 32, 128), F32),
            pltpu.VMEM((NT * 16, 128), F32),
            pltpu.VMEM((1024, 128), F32),
            pltpu.VMEM((1024, 1024), BF16),
            pltpu.VMEM((512, 2048), BF16),
            pltpu.VMEM((64, 2048), BF16),
            pltpu.VMEM((NT, 32, 128), BF16),
            pltpu.VMEM((NT, 32, 128), BF16),
            pltpu.VMEM((NT, 16, 128), BF16),
            pltpu.VMEM((NT, 16, 128), BF16),
            pltpu.VMEM((NT, 2, 128), F32),
            pltpu.VMEM((NT, 2, 128), F32),
            pltpu.VMEM((16, 64, 128), BF16),
            pltpu.VMEM((16, 64, 128), BF16),
            pltpu.VMEM((16, 48, 128), BF16),
            pltpu.VMEM((16, 48, 128), BF16),
            pltpu.VMEM((16, 16, 512), BF16),
            pltpu.VMEM((16, 16, 512), BF16),
            pltpu.VMEM((1024, 128), F32),
            pltpu.VMEM((768, 128), F32),
            dma((len(inputs),)),
            *([dma] * 16),
        ],
        compiler_params=pltpu.CompilerParams(
            collective_id=0, has_side_effects=True, vmem_limit_bytes=36 * 1024 * 1024
        ),
        name="exchange",
    )(*(pltpu.with_memory_space_constraint(a, pltpu.HBM) for a in inputs))
    return pl.pallas_call(
        head_product,
        out_shape=(
            jax.ShapeDtypeStruct((H, 512), BF16),
            jax.ShapeDtypeStruct((H, 256), BF16),
            jax.ShapeDtypeStruct((H // NS, 256), BF16),
        ),
        in_specs=[vmem] * 4,
        out_specs=(hbm,) * 3,
        scratch_shapes=[
            pltpu.VMEM((H, 256), BF16),
            pltpu.VMEM((H // NS, 256), BF16),
            dma((2 * PIECES + 1,)),
        ],
        compiler_params=pltpu.CompilerParams(vmem_limit_bytes=20 * 1024 * 1024),
        name="head_product",
    )(head, prod_a, s_q.reshape(256, 512), head_own)


def solution(mesh):
    placed = (
        P("section", "tensor", None),
        P("section", "tensor", None),
        P("section", "tensor", None),
        P("section", None, "tensor"),
        P("section", None, "tensor"),
        P("section", None, "tensor"),
        P("section", None),
        P(),
        P(),
        P(),
        P(),
    )
    return jax.shard_map(
        shards,
        mesh=mesh,
        in_specs=placed,
        out_specs=(
            P(None, ("tensor", "section")),
            P(None, ("tensor", "section")),
            P("section", "tensor"),
        ),
        check_vma=False,
    )
```

```python
import functools
import math

import jax
import jax.numpy as jnp
from jax import lax
from jax.experimental import pallas as pl
from jax.experimental.pallas import tpu as pltpu
from jax.sharding import PartitionSpec as P

MESH = pl.DeviceIdType.MESH
F32, BF16 = jnp.float32, jnp.bfloat16

H = 4096
R = 8
TENANTS = 128
TASKS = 32
LAYERS = 80
TOK = 128
NS, NT = 8, 32
NX, NY, NZL, NZH, NC = 4, 4, 4, 2, 2
HEAD_FIRST = 10
PIECES = 4
SCALE = 2.0 / math.sqrt(TOK * NT * NS)


def mm(a, b):
    return jnp.dot(a, b, preferred_element_type=F32)


def each(first, last, body):
    for k in range(first, last):
        body(k, 0)


def all_in(slots, count, sem):
    some = slots.at[pl.ds(0, count)]
    pltpu.make_async_copy(some, some, sem).wait()


def iota(shape, dim):
    return lax.broadcasted_iota(jnp.int32, shape, dim)


def exchange(
    acts, gq, gv, fa, fq, fv, own, task_of, layer_of, task_emb, layer_emb,
    s_a, s_q, head, head_own, prod_a,
    acts_v, gq_v, gv_v, fa_v, fq_v, fv_v, emb_v, own_v, task_v, layer_v,
    own_s, own_r, gat_a, gat_q, tr, a2, b2, v2,
    p_as, p_ar, p_qs, p_qr, p_vs, p_vr, z_as, z_ar, z_qs, z_qr, x_as, x_qs, big_a, big_q,
    load_sem, own_ss, own_rs, pa_ss, pa_rs, pq_ss, pq_rs, pv_ss, pv_rs, za_ss, za_rs, zq_ss, zq_rs, xa_ss, xa_rs, xq_ss, xq_rs,
):
    s, t = lax.axis_index("section"), lax.axis_index("tensor")
    y, zh = lax.div(s, 2), lax.rem(s, 2)
    zl, x, c = lax.div(t, 8), lax.rem(lax.div(t, 2), 4), lax.rem(t, 2)
    zdev = (zl * 2 + zh) * 2 + c
    xy = x * 4 + y

    def around(j, half):
        return half + (j + 1) // 2 * (1 - 2 * (j % 2))

    def tensor_peer(k):
        return lax.rem(t + around(k, NT // 2), NT)

    def z_peer(k):
        z = lax.rem(zh * 4 + zl + around(k // 2, 4), 8)
        to_c = lax.rem(c + 1 - (k % 2), 2)
        to_zh = lax.div(z, 4)
        to_zl = z - 4 * to_zh
        return (to_zl * 2 + to_zh) * 2 + to_c, (y * 2 + to_zh, (to_zl * 4 + x) * 2 + to_c)

    def xy_peer(k):
        to_x, to_y = lax.rem(x + around(k // 4, 2), 4), lax.rem(y + around(k % 4, 2), 4)
        return to_x * 4 + to_y, (to_y * 2 + zh, (zl * 4 + to_x) * 2 + c)

    loads = [
        pltpu.make_async_copy(src, dst, load_sem.at[i])
        for i, (src, dst) in enumerate(
            (
                (own, own_v), (fq, fq_v), (fv, fv_v), (fa, fa_v), (gq, gq_v), (gv, gv_v), (acts, acts_v),
                (task_emb, emb_v.at[pl.ds(0, TASKS)]),
                (layer_emb, emb_v.at[pl.ds(TASKS, LAYERS)]),
                (task_of, task_v), (layer_of, layer_v),
            )
        )
    ]
    for load in loads[:4]:
        load.start()

    bar = pltpu.get_barrier_semaphore()

    def greet(section, tensor):
        pl.semaphore_signal(bar, inc=1, device_id=(section, tensor), device_id_type=MESH)

    def greet_z(k, _):
        greet(y * 2 + 1 - zh, ((k // 2) * 4 + x) * 2 + (k % 2))
        return 0

    each(0, NZL * NC, greet_z)

    def greet_xy(k, _):
        greet(lax.rem(y + 1 + (k // 4), NY) * 2 + zh, (zl * 4 + (k % 4)) * 2 + c)
        return 0

    each(0, (NY - 1) * NX, greet_xy)

    def greet_far(k, _):
        greet(lax.rem(y + k, NY) * 2 + 1 - zh, t)
        return 0

    each(1, NY, greet_far)

    def greet_tensor(k, _):
        greet(s, tensor_peer(k))
        return 0

    each(0, NT - 1, greet_tensor)

    for load in loads[4:]:
        load.start()

    loads[0].wait()
    mine = own_v[...]
    hot_t = (iota((TENANTS, NT), 0) == mine).astype(F32).astype(BF16)

    def pick(block):
        return lax.dot_general(hot_t, block, (((0,), (0,)), ((), ())), preferred_element_type=F32)

    loads[1].wait()
    loads[2].wait()
    for i in range(8):
        got = pick(fq_v[:, i * 256 : (i + 1) * 256])
        for h in range(2):
            yy, zz = i // 2, i % 2
            gat_q[pl.ds(zz * 8 + yy * 2 + h, NT, stride=16), :] = got[:, h * 128 : (h + 1) * 128]
    got = pick(fv_v[...])
    for h in range(2):
        p_vs[:, h, :] = got[:, h * 128 : (h + 1) * 128]
    p_vr[pl.ds(t, 1)] = p_vs[pl.ds(t, 1)]
    p_qs[...] = gat_q[...].reshape(NT, 16, 128).astype(BF16)
    p_qr[pl.ds(t, 1)] = p_qs[pl.ds(t, 1)]

    own_s[...] = jnp.concatenate([mine.astype(F32), jnp.zeros((1, 96), F32)], axis=1)
    own_r[pl.ds(s, 1)] = own_s[...].reshape(1, 1, 128)

    pl.semaphore_wait(bar, (NT - 1) + NZL * NC + (NY - 1) * NX + NY - 1)

    def factor_copy(k, src, dst, send, recv):
        to = tensor_peer(k)
        return pltpu.make_async_remote_copy(
            src_ref=src.at[to], dst_ref=dst.at[t], send_sem=send, recv_sem=recv,
            device_id=(s, to), device_id_type=MESH,
        )

    def own_copy(k):
        to = lax.rem(s + k, NS)
        return pltpu.make_async_remote_copy(
            src_ref=own_s, dst_ref=own_r.at[s], send_sem=own_ss, recv_sem=own_rs,
            device_id=(to, t), device_id_type=MESH,
        )

    def send_own(k, _):
        own_copy(k).start()
        return 0


    def send_q(k, _):
        factor_copy(k, p_vs, p_vr, pv_ss, pv_rs).start()
        factor_copy(k, p_qs, p_qr, pq_ss, pq_rs).start()
        return 0

    each(0, NT - 1, send_q)

    loads[3].wait()
    for i in range(16):
        got = pick(fa_v[:, i * 256 : (i + 1) * 256])
        for h in range(2):
            n = i * 2 + h
            yy, zz, rr = n // 8, (n // 4) % 2, n % 4
            gat_a[pl.ds(zz * 16 + yy * 4 + rr, NT, stride=32), :] = got[:, h * 128 : (h + 1) * 128]
    p_as[...] = gat_a[...].reshape(NT, 32, 128).astype(BF16)
    p_ar[pl.ds(t, 1)] = p_as[pl.ds(t, 1)]

    def send_a(k, _):
        factor_copy(k, p_as, p_ar, pa_ss, pa_rs).start()
        return 0

    each(0, NT - 1, send_a)
    each(1, NS, send_own)

    loads[4].wait()

    def turn_q(i, _):
        zl_, c_, xp = i // 4, (i // 2) % 2, i % 2
        base = pl.multiple_of((i % 2) * 512, 512)
        for xi in range(2):
            tt = (zl_ * 4 + xp * 2 + xi) * 2 + c_
            for h in range(2):
                block = gq_v[:, pl.ds(pl.multiple_of(tt * 256 + h * 128, 128), 128)].astype(F32).T
                for yy in range(2):
                    for zz in range(2):
                        tr[pl.ds(base + zz * 256 + xi * 128 + (2 * h + yy) * 32, 32), :] = block[
                            (yy * 2 + zz) * 32 : (yy * 2 + zz + 1) * 32
                        ]
        for zz in range(2):
            row = pl.multiple_of(((zl_ * 2 + zz) * 2 + c_) * 32 + xp * 16, 16)
            for e in range(16):
                b2[pl.ds(row, 16), e * 128 : (e + 1) * 128] = tr[
                    pl.ds(base + zz * 256 + e, 16, stride=16), :
                ].astype(BF16)
        return 0

    lax.fori_loop(0, 16, turn_q, 0, unroll=2)

    loads[5].wait()
    for zl_ in range(4):
        for h in range(2):
            block = gv_v[:, (zl_ * 2 + h) * 128 : (zl_ * 2 + h + 1) * 128].astype(F32).T
            for xx in range(2):
                for c_ in range(2):
                    to = (zl_ * 2 + c_) * 128 + (2 * h + xx) * 32
                    tr[to : to + 32, :] = block[(xx * 2 + c_) * 32 : (xx * 2 + c_ + 1) * 32]
    for g in range(4):
        for e in range(16):
            v2[g * 16 : (g + 1) * 16, e * 128 : (e + 1) * 128] = tr[pl.ds(g * 256 + e, 16, stride=16), :].astype(BF16)

    loads[6].wait()

    def turn_a(i, _):
        base = pl.multiple_of((i % 4) * 256, 256)
        zl_, x_, c_ = i // 8, (i // 2) % 4, i % 2
        for h in range(2):
            block = acts_v[:, pl.ds(pl.multiple_of(i * 256 + h * 128, 128), 128)].astype(F32).T
            for yy in range(2):
                for zz in range(2):
                    tr[pl.ds(base + zz * 128 + (2 * h + yy) * 32, 32), :] = block[
                        (yy * 2 + zz) * 32 : (yy * 2 + zz + 1) * 32
                    ]
        for zz in range(2):
            row = pl.multiple_of((((zl_ * 2 + zz) * 2 + c_) * 4 + x_) * 16, 16)
            for d in range(8):
                a2[pl.ds(row, 16), d * 128 : (d + 1) * 128] = tr[pl.ds(base + zz * 128 + d, 16, stride=8), :].astype(BF16)
        return 0

    lax.fori_loop(0, 32, turn_a, 0, unroll=4)

    all_in(p_vr, NT - 1, pv_rs)
    all_in(p_qr, NT - 1, pq_rs)

    places = [(zl_, zz, c_, x_) for zl_ in range(4) for zz in range(2) for c_ in range(2) for x_ in range(4)]
    backq = jnp.zeros((R, TOK), F32)
    fq_rows = jnp.concatenate(
        [p_qr[(zl_ * 4 + x_) * 2 + c_, 0:16, :].astype(F32)[zz * 8 : (zz + 1) * 8] for zl_, zz, c_, x_ in places], axis=0
    )
    fq_t = fq_rows.T.astype(BF16)
    for n in range(8):
        part = mm(fq_t[n * 16 : (n + 1) * 16], b2[:, n * 256 : (n + 1) * 256])
        backq = backq + part[0:8, 0:128] + part[8:16, 128:256]
    fv_rows = jnp.concatenate(
        [p_vr[(zl_ * 4 + x_) * 2 + c_] for zl_ in range(4) for c_ in range(2) for x_ in range(4)],
        axis=0,
    )
    fv_t = jnp.concatenate([fv_rows, jnp.zeros((64, 128), F32)], axis=0).T.astype(BF16)[:, 0:64]
    backv = jnp.zeros((R, TOK), F32)
    for n in range(8):
        part = mm(fv_t[n * 16 : (n + 1) * 16], v2[:, n * 256 : (n + 1) * 256])
        backv = backv + part[0:8, 0:128] + part[8:16, 128:256]
    back_t = jnp.concatenate([backq, backv], axis=0).astype(BF16).astype(F32)
    back = jnp.concatenate([back_t] * 8, axis=0).T
    lane = iota((TOK, 128), 1)
    diag = jnp.concatenate([jnp.where(lane // 16 == d, back, 0.0).astype(BF16) for d in range(8)], axis=0)

    def z_copy(k, src, dst, send, recv):
        q, device = z_peer(k)
        return pltpu.make_async_remote_copy(
            src_ref=src.at[q], dst_ref=dst.at[zdev], send_sem=send, recv_sem=recv,
            device_id=device, device_id_type=MESH,
        )

    for n in range(4):
        z_as[n * 4 : (n + 1) * 4] = (SCALE * mm(a2[n * 256 : (n + 1) * 256, :], diag)).astype(BF16).reshape(4, 64, 128)

    def send_za(k, _):
        z_copy(k, z_as, z_ar, za_ss, za_rs).start()
        return 0

    each(0, 15, send_za)
    z_ar[pl.ds(zdev, 1)] = z_as[pl.ds(zdev, 1)]

    all_in(own_r, NS - 1, own_rs)
    for i in (7, 8, 9, 10):
        loads[i].wait()
    n_seq = NS * NT
    col = iota((1, n_seq), 1)
    col_s = (col // 16 % 4) * 2 + (col // 2) % 2
    col_t = ((col // 4 % 4) * 4 + col // 64) * 2 + col % 2
    owners = jnp.concatenate([own_r[i] for i in range(NS)], axis=0)
    spread = mm(owners.astype(BF16), (iota((128, n_seq), 0) == col_t).astype(F32).astype(BF16))
    in_section = iota((NS, n_seq), 0) == col_s
    tenant = jnp.sum(jnp.where(in_section, spread, 0.0), axis=0, keepdims=True)
    hot_tenant = (iota((TENANTS, n_seq), 0).astype(F32) == tenant).astype(F32).astype(BF16)
    tasks = jnp.broadcast_to(task_v[...].astype(F32), (8, TENANTS)).astype(BF16)
    task = mm(tasks, hot_tenant)[0:1]
    layers = jnp.broadcast_to(layer_v[...].astype(F32), (NS, NS)).astype(BF16)
    layer = mm(layers, in_section.astype(F32).astype(BF16))[0:1]
    row = iota((TASKS + LAYERS, n_seq), 0).astype(F32)
    hot_head = (row == jnp.where(row < TASKS, task, layer + TASKS)).astype(F32).astype(BF16)

    def head_block(i, _):
        at = pl.multiple_of(i * 256, 256)
        v = lax.dot_general(
            emb_v[:, pl.ds(at, 256)], hot_head, (((0,), (0,)), ((), ())), preferred_element_type=F32
        )
        head[pl.ds(at, 256), :] = (v / (1.0 + jnp.exp(-v))).astype(BF16)
        return 0

    lax.fori_loop(0, HEAD_FIRST, head_block, 0)

    all_in(p_ar, NT - 1, pa_rs)
    fa_rows = jnp.concatenate([p_ar[(zl_ * 4 + x_) * 2 + c_, zz * 16 : (zz + 1) * 16, :] for zl_, zz, c_, x_ in places], axis=0)
    fa_t = fa_rows.astype(F32).T.astype(BF16)
    down_t = jnp.zeros((2 * R, TOK), F32)
    for n in range(4):
        part = mm(fa_t[n * 32 : (n + 1) * 32], a2[:, n * 256 : (n + 1) * 256])
        down_t = down_t + part[0:16, 0:128] + part[16:32, 128:256]
    down_t = down_t.astype(BF16).astype(F32)
    down_q = jnp.concatenate([down_t[0:8]] * 16, axis=0).T
    down_v = jnp.concatenate([down_t[8:16]] * 16, axis=0).T
    diag_q = jnp.concatenate([jnp.where(lane // 8 == e, down_q, 0.0).astype(BF16) for e in range(16)], axis=0)
    diag_v = jnp.concatenate([jnp.where(lane // 8 == e, down_v, 0.0).astype(BF16) for e in range(16)], axis=0)
    grad_v_rows = SCALE * mm(v2[...], diag_v)
    grad_v_rows = jnp.concatenate([grad_v_rows.reshape(8, 8, 128), jnp.zeros((8, 8, 128), F32)], axis=1).astype(BF16)
    grad_q_rows = (SCALE * mm(b2[...], diag_q)).astype(BF16).reshape(16, 32, 128)
    for q in range(16):
        z_qs[q, 0:32, :] = grad_q_rows[q]
        z_qs[q, 32:48, :] = grad_v_rows[(q // 4) * 2 + q % 2]

    def send_zq(k, _):
        z_copy(k, z_qs, z_qr, zq_ss, zq_rs).start()
        return 0

    each(0, 15, send_zq)
    z_qr[pl.ds(zdev, 1)] = z_qs[pl.ds(zdev, 1)]

    lax.fori_loop(HEAD_FIRST, H // 256, head_block, 0)
    share = H // NS
    head_own[...] = head[pl.ds(pl.multiple_of(s * share, share), share), :]

    def xy_copy(k, src, dst, send, recv):
        b, device = xy_peer(k)
        return pltpu.make_async_remote_copy(
            src_ref=src.at[b], dst_ref=dst.at[xy], send_sem=send, recv_sem=recv,
            device_id=device, device_id_type=MESH,
        )

    all_in(z_ar, 15, za_rs)
    big_a[...] = z_ar[...].astype(F32).reshape(1024, 128)
    for b in range(16):
        for i in range(4):
            x_as[b, :, i * 128 : (i + 1) * 128] = big_a[pl.ds(b * 4 + i, 16, stride=64), :].astype(BF16)

    def send_xa(k, _):
        xy_copy(k, x_as, s_a, xa_ss, xa_rs).start()
        return 0

    each(0, 15, send_xa)
    s_a[pl.ds(xy, 1)] = x_as[pl.ds(xy, 1)]

    all_in(z_qr, 15, zq_rs)
    big_q[...] = z_qr[...].astype(F32).reshape(768, 128)
    for b in range(16):
        for i in range(2):
            x_qs[b, :, i * 128 : (i + 1) * 128] = big_q[pl.ds(b * 2 + i, 16, stride=48), :].astype(BF16)
            x_qs[b, :, 256 + i * 128 : 256 + (i + 1) * 128] = big_q[
                pl.ds(32 + (b // 4) * 2 + i, 16, stride=48), :
            ].astype(BF16)

    def send_xq(k, _):
        xy_copy(k, x_qs, s_q, xq_ss, xq_rs).start()
        return 0

    each(0, 15, send_xq)
    s_q[pl.ds(xy, 1)] = x_qs[pl.ds(xy, 1)]

    all_in(s_a, 15, xa_rs)

    def product(i, _):
        at = pl.ds(pl.multiple_of(i * 512, 512), 512)
        prod_a[at, :] = mm(head[at, :], s_a[...].reshape(256, 512)).astype(BF16)
        return 0

    lax.fori_loop(0, H // 512, product, 0)

    all_in(p_vs, NT - 1, pv_ss)
    all_in(p_qs, NT - 1, pq_ss)
    all_in(p_as, NT - 1, pa_ss)

    all_in(own_r, NS - 1, own_ss)

    all_in(z_as, 15, za_ss)
    all_in(z_qs, 15, zq_ss)

    all_in(x_as, 15, xa_ss)
    all_in(x_qs, 15, xq_ss)

    all_in(s_q, 15, xq_rs)


def head_product(head, prod_a, s_q, head_own, grad_a, grad_bq, grad_bv, q_v, v_v, sem):
    copies = []

    def write(src, dst, rows):
        copy = pltpu.make_async_copy(src.at[rows], dst.at[rows], sem.at[len(copies)])
        copy.start()
        copies.append(copy)

    step = H // PIECES
    for p in range(PIECES):
        write(prod_a, grad_a, pl.ds(p * step, step))
    for p in range(PIECES):
        for r in range(p * step, (p + 1) * step, 256):
            q_v[r : r + 256, :] = mm(head[r : r + 256, :], s_q[:, 0:256]).astype(BF16)
        write(q_v, grad_bq, pl.ds(p * step, step))
    v_v[...] = mm(head_own[...], s_q[:, 256:512]).astype(BF16)
    write(v_v, grad_bv, pl.ds(0, H // NS))
    for copy in copies:
        copy.wait()


def shards(acts, grad_q, grad_v, fac_a, fac_bq, fac_bv, seq_tenant, tenant_task, section_layer, task_emb, layer_emb):
    vmem = pl.BlockSpec(memory_space=pltpu.VMEM)
    hbm = pl.BlockSpec(memory_space=pltpu.HBM)
    dma = pltpu.SemaphoreType.DMA
    inputs = (
        acts[0], grad_q[0], grad_v[0], fac_a[0], fac_bq[0], fac_bv[0], seq_tenant,
        tenant_task.reshape(1, TENANTS), section_layer.reshape(1, NS), task_emb, layer_emb,
    )
    _, s_q, head, head_own, prod_a = pl.pallas_call(
        exchange,
        out_shape=(
            pltpu.VMEM((16, 16, 512), BF16),
            pltpu.VMEM((16, 16, 512), BF16),
            pltpu.VMEM((H, NS * NT), BF16),
            pltpu.VMEM((H // NS, NS * NT), BF16),
            pltpu.VMEM((H, 512), BF16),
        ),
        in_specs=[hbm] * len(inputs),
        out_specs=(vmem,) * 5,
        scratch_shapes=[
            pltpu.VMEM((TOK, 8192), BF16),
            pltpu.VMEM((TOK, 8192), BF16),
            pltpu.VMEM((TOK, 1024), BF16),
            pltpu.VMEM((TENANTS, 4096), BF16),
            pltpu.VMEM((TENANTS, 2048), BF16),
            pltpu.VMEM((TENANTS, 256), BF16),
            pltpu.VMEM((TASKS + LAYERS, H), BF16),
            pltpu.VMEM((1, NT), jnp.int32),
            pltpu.VMEM((1, TENANTS), jnp.int32),
            pltpu.VMEM((1, NS), jnp.int32),
            pltpu.VMEM((1, 128), F32),
            pltpu.VMEM((NS, 1, 128), F32),
            pltpu.VMEM((NT * 32, 128), F32),
            pltpu.VMEM((NT * 16, 128), F32),
            pltpu.VMEM((1024, 128), F32),
            pltpu.VMEM((1024, 1024), BF16),
            pltpu.VMEM((512, 2048), BF16),
            pltpu.VMEM((64, 2048), BF16),
            pltpu.VMEM((NT, 32, 128), BF16),
            pltpu.VMEM((NT, 32, 128), BF16),
            pltpu.VMEM((NT, 16, 128), BF16),
            pltpu.VMEM((NT, 16, 128), BF16),
            pltpu.VMEM((NT, 2, 128), F32),
            pltpu.VMEM((NT, 2, 128), F32),
            pltpu.VMEM((16, 64, 128), BF16),
            pltpu.VMEM((16, 64, 128), BF16),
            pltpu.VMEM((16, 48, 128), BF16),
            pltpu.VMEM((16, 48, 128), BF16),
            pltpu.VMEM((16, 16, 512), BF16),
            pltpu.VMEM((16, 16, 512), BF16),
            pltpu.VMEM((1024, 128), F32),
            pltpu.VMEM((768, 128), F32),
            dma((len(inputs),)),
            *([dma] * 16),
        ],
        compiler_params=pltpu.CompilerParams(
            collective_id=0, has_side_effects=True, vmem_limit_bytes=36 * 1024 * 1024
        ),
        name="exchange",
    )(*(pltpu.with_memory_space_constraint(a, pltpu.HBM) for a in inputs))
    return pl.pallas_call(
        head_product,
        out_shape=(
            jax.ShapeDtypeStruct((H, 512), BF16),
            jax.ShapeDtypeStruct((H, 256), BF16),
            jax.ShapeDtypeStruct((H // NS, 256), BF16),
        ),
        in_specs=[vmem] * 4,
        out_specs=(hbm,) * 3,
        scratch_shapes=[
            pltpu.VMEM((H, 256), BF16),
            pltpu.VMEM((H // NS, 256), BF16),
            dma((2 * PIECES + 1,)),
        ],
        compiler_params=pltpu.CompilerParams(vmem_limit_bytes=20 * 1024 * 1024),
        name="head_product",
    )(head, prod_a, s_q.reshape(256, 512), head_own)


def solution(mesh):
    placed = (
        P("section", "tensor", None),
        P("section", "tensor", None),
        P("section", "tensor", None),
        P("section", None, "tensor"),
        P("section", None, "tensor"),
        P("section", None, "tensor"),
        P("section", None),
        P(),
        P(),
        P(),
        P(),
    )
    return jax.shard_map(
        shards,
        mesh=mesh,
        in_specs=placed,
        out_specs=(
            P(None, ("tensor", "section")),
            P(None, ("tensor", "section")),
            P("section", "tensor"),
        ),
        check_vma=False,
    )
```
